32 devices in a mesh: experts: 8 (over z, y), context: 2 (over x), dp: 2 (over core).
Axes of the slice: x: 2, y: 2, z: 4, core: 2. Of those that a mesh axis runs over, the one named last changes fastest.
Arguments:
- layer_input: bfloat16 [2, 2, 1024, 2048], P('dp', 'context'), may hold values from -6 to 6
- routes: int32 [2, 2, 1024, 6], P('dp', 'context'), may hold values from 0 to 15, all different within a row; in each aligned block of 1024 rows (0 to 1023, 1024 to 2047, ..., all dimensions but the last counted through in order) at most 512 rows name the same one
- route_weights: float32 [2, 2, 1024, 6], P('dp', 'context'), may hold values from 0.05 to 0.3
- query_weight: bfloat16 [2048, 3072], P(None, 'experts'), may hold values from -0.125 to 0.125
- latent_weight: bfloat16 [2048, 576], replicated, may hold values from -0.125 to 0.125
- keyval_weight: bfloat16 [512, 4096], P(None, 'experts'), may hold values from -0.25 to 0.25
- output_weight: bfloat16 [2048, 2048], P('experts'), may hold values from -0.5 to 0.5
- attn_gain: float32 [2048], replicated, may hold values from 0.25 to 1.75
- latent_gain: float32 [512], replicated, may hold values from 0.25 to 1.75
- ffn_gain: float32 [2048], replicated, may hold values from 0.25 to 1.75
- shared_gate: bfloat16 [2048, 2816], P(None, 'experts'), may hold values from -0.125 to 0.125
- shared_up: bfloat16 [2048, 2816], P(None, 'experts'), may hold values from -0.125 to 0.125
- shared_down: bfloat16 [2816, 2048], P('experts'), may hold values from -0.109375 to 0.109375
- expert_gate: bfloat16 [16, 2048, 1408], P('experts', ('context', 'dp')), may hold values from -0.125 to 0.125
- expert_up: bfloat16 [16, 2048, 1408], P('experts', ('context', 'dp')), may hold values from -0.125 to 0.125
- expert_down: bfloat16 [16, 1408, 2048], P('experts', None, ('context', 'dp')), may hold values from -0.15625 to 0.15625
- cotangent: bfloat16 [2, 2, 1024, 2048], P('dp', 'context'), may hold values from -6 to 6
Outputs:
- layer_output: bfloat16 [2, 2, 1024, 2048], P('dp', 'context', 'experts')
- input_grad: float32 [2, 2, 1024, 2048], P('dp', 'context', 'experts')
- query_grad: float32 [2048, 3072], P(None, 'experts')
- latent_grad: float32 [2048, 576], replicated
- keyval_grad: float32 [512, 4096], P(None, 'experts')
- output_grad: float32 [2048, 2048], P('experts')
- attn_gain_grad: float32 [2048], replicated
- latent_gain_grad: float32 [512], replicated
- ffn_gain_grad: float32 [2048], replicated
- shared_gate_grad: float32 [2048, 2816], P(None, 'experts')
- shared_up_grad: float32 [2048, 2816], P(None, 'experts')
- shared_down_grad: float32 [2816, 2048], P('experts')
- expert_gate_grad: float32 [16, 2048, 1408], P('experts', ('context', 'dp'))
- expert_up_grad: float32 [16, 2048, 1408], P('experts', ('context', 'dp'))
- expert_down_grad: float32 [16, 1408, 2048], P('experts', None, ('context', 'dp'))
The draws below stay inside these ranges and needn't reach their ends.
Inputs may be any that keep to these rules, and one draw needn't show every extreme that they name: `routes`: each row names 6 different experts. Within the 1024 rows of one block of a sequence no expert is named by more than 512 rows, and in some block one expert is named by exactly 512.
All inputs are finite; a program needn't handle non-finite values.
Results may differ from the reference program's by a relative error of at most 0.022.
Values may be sent and summed in bfloat16 or wider, within the bound.
No kernel may reach another device: no remote copies, remote signals or barrier semaphores. Data moves between devices by JAX's collectives and lax.ppermute only.
A program may use at most 384 MiB of HBM per device.

```python
import math
import jax
import jax.numpy as jnp
import numpy as np
from jax import lax

D = 2048
HEADS = 16
NOPE = 128
ROPE = 64
VDIM = 128
RANK = 512
FF = 1408
SHARED = 2816
TOPK = 6
EXPERTS = 16
BLOCK = 1024
LEN = 2048
SEQS = 2
CAPB = 512
N_CONTEXT = 2


def block_scale(key, extent, shards, least, top_value):
    level = 1.0
    for axis_at, parts in shards:
        draws = jax.random.uniform(jax.random.fold_in(jax.random.fold_in(key, 6), axis_at), (parts,), jnp.float32, least / len(shards), top_value / len(shards))
        level = level * jnp.repeat(jnp.exp(draws), extent[axis_at] // parts).reshape((-1,) + (1,) * (len(extent) - 1 - axis_at))
    return level


def assign_block(rng, own, number, rows, amount, top, most, slope):
    order = jax.random.permutation(rng, amount)
    heavy_load, ordinary = shares(amount, rows * top, most, slope, True), shares(amount, rows * top, most, slope, False)
    places = jnp.arange(amount)

    def named(sizes, offset_by):
        used = int((sizes > 0).sum())
        fixed = max(1, used // 4)
        shifted = fixed + (places - fixed + offset_by * (used - fixed)) % max(1, amount - fixed)
        return jnp.zeros((amount,), jnp.int32).at[order[jnp.where(places < fixed, places, shifted)]].set(jnp.asarray(sizes, jnp.int32))

    sizes = jnp.where(number % 4 == 0, named(heavy_load, number // 4), named(ordinary, number - number // 4 - 1))
    mixed = jax.random.permutation(jax.random.fold_in(own, 3), amount)
    donor, taker = mixed[0:amount // 2 * 2:2], mixed[1:amount // 2 * 2:2]
    slack = jnp.minimum(sizes[donor] - 1, most - sizes[taker]) // 2
    slack = jnp.where((donor == order[0]) | (taker == order[0]) | (sizes[taker] == 0), 0, jnp.maximum(slack, 0))
    shifted = jax.random.randint(jax.random.fold_in(own, 4), (amount // 2,), 0, 1 << 20) % (slack + 1)
    sizes = sizes.at[donor].add(-shifted).at[taker].add(shifted)
    items = jnp.searchsorted(jnp.cumsum(sizes), jnp.arange(rows * top), side="right").astype(jnp.int32)
    grid = items.reshape(top, rows).T
    grid = grid[jax.random.permutation(jax.random.fold_in(own, 1), rows)]
    offset_by = jax.random.randint(jax.random.fold_in(own, 2), (rows, 1), 0, top)
    return jnp.take_along_axis(grid, (jnp.arange(top)[None, :] + offset_by) % top, axis=1)


def shares(amount, total, limit, lean, full):
    weights = [(1 << 20) // math.isqrt(standing ** lean) + 1 for standing in range(1, amount + 1)]
    largest = limit if full else min(limit, max(-(-total // amount), total * weights[0] // sum(weights)))
    least = 1 if total - largest >= amount - 1 else 0
    holding, rest = [largest] + [least] * (amount - 1), total - largest - least * (amount - 1)
    while rest > 0:
        movable = [i for i in range(1, amount) if holding[i] < largest] or [i for i in range(1, amount) if holding[i] < limit]
        pool, budget = sum([weights[i] for i in movable]), rest
        for i in movable:
            addition = min(limit - holding[i], max(1, budget * weights[i] // pool), rest)
            holding[i] = holding[i] + addition
            rest = rest - addition
    return np.array(holding)


def noise(key, extent, scale, reach, cuts=(), held_as=jnp.bfloat16):
    loudness = block_scale(key, extent, cuts, -0.22, 0.18) if cuts else 1.0
    values = jax.random.normal(key, extent, jnp.float32) * scale * loudness
    return jnp.minimum(jnp.maximum(values, -reach), reach).astype(held_as)


def setup_inputs(seed: int = 0) -> dict:
    splits = jax.random.split(jax.random.key(seed), 18)
    layer_input = noise(splits[0], (SEQS, N_CONTEXT, BLOCK, D), 1.0, 6.0, ((0, 2), (1, 2)))
    routes_keys = jax.random.split(jax.random.fold_in(splits[1], 1), SEQS * N_CONTEXT * BLOCK // BLOCK)
    routes_turns = jax.random.permutation(jax.random.fold_in(splits[1], 3), SEQS * N_CONTEXT * BLOCK // BLOCK)
    routes = jax.vmap(lambda own, number: assign_block(jax.random.fold_in(splits[1], 2), own, number, BLOCK, EXPERTS, TOPK, CAPB, 1))(routes_keys, routes_turns).reshape((SEQS, N_CONTEXT, BLOCK, TOPK))
    route_weights = jnp.clip(0.05 + 0.25 * jax.random.uniform(splits[2], (SEQS, N_CONTEXT, BLOCK, TOPK), jnp.float32) ** block_scale(splits[2], (SEQS, N_CONTEXT, BLOCK, TOPK), ((0, 2), (1, 2)), -0.2, 0.2), 0.05, 0.3)
    query_weight = noise(splits[3], (D, HEADS * (NOPE + ROPE)), D ** -0.5, 0.125, ((1, 8),))
    latent_weight = noise(splits[4], (D, RANK + ROPE), D ** -0.5, 0.125)
    keyval_weight = noise(splits[5], (RANK, HEADS * (NOPE + VDIM)), RANK ** -0.5, 0.25, ((1, 8),))
    output_weight = noise(splits[6], (HEADS * VDIM, D), (HEADS * VDIM // 16) ** -0.5, 0.5, ((0, 8),))
    attn_gain = jnp.clip(1.0 + 0.15 * jax.random.normal(splits[7], (D,), jnp.float32), 0.25, 1.75)
    latent_gain = jnp.clip(1.0 + 0.15 * jax.random.normal(splits[8], (RANK,), jnp.float32), 0.25, 1.75)
    ffn_gain = jnp.clip(1.0 + 0.15 * jax.random.normal(splits[9], (D,), jnp.float32), 0.25, 1.75)
    shared_gate = noise(splits[10], (D, SHARED), D ** -0.5, 0.125, ((1, 8),))
    shared_up = noise(splits[11], (D, SHARED), D ** -0.5, 0.125, ((1, 8),))
    shared_down = noise(splits[12], (SHARED, D), SHARED ** -0.5, 0.109375, ((0, 8),))
    expert_gate = noise(splits[13], (EXPERTS, D, FF), D ** -0.5, 0.125, ((0, 8), (1, 4)))
    expert_up = noise(splits[14], (EXPERTS, D, FF), D ** -0.5, 0.125, ((0, 8), (1, 4)))
    expert_down = noise(splits[15], (EXPERTS, FF, D), FF ** -0.5, 0.15625, ((0, 8), (2, 4)))
    cotangent = noise(splits[16], (SEQS, N_CONTEXT, BLOCK, D), 1.0, 6.0, ((0, 2), (1, 2)))
    return {"layer_input": layer_input, "routes": routes, "route_weights": route_weights, "query_weight": query_weight, "latent_weight": latent_weight, "keyval_weight": keyval_weight, "output_weight": output_weight, "attn_gain": attn_gain, "latent_gain": latent_gain, "ffn_gain": ffn_gain, "shared_gate": shared_gate, "shared_up": shared_up, "shared_down": shared_down, "expert_gate": expert_gate, "expert_up": expert_up, "expert_down": expert_down, "cotangent": cotangent}


EPSILON = 1e-06
ROPE_BASE = 50000.0
MASKED = -1e+30
HIGH = lax.Precision.HIGHEST

@jax.custom_vjp
def low(v):
    return lax.optimization_barrier(v.astype(jnp.bfloat16)).astype(jnp.float32)

@jax.custom_vjp
def low_back(v):
    return v

def low_keep(v):
    return (low(v), None)

def low_pass(kept, grad):
    return (grad,)

def back_keep(v):
    return (v, None)

def back_low(kept, grad):
    return (low(grad),)
low.defvjp(low_keep, low_pass)
low_back.defvjp(back_keep, back_low)

def angles(positions):
    half_width = ROPE // 2
    freqs_table = ROPE_BASE ** (-jnp.arange(half_width, dtype=jnp.float32) * 2.0 / ROPE)
    turned = positions.astype(jnp.float32)[:, None] * freqs_table[None, :]
    return (jnp.cos(turned), jnp.sin(turned))

def rotate(values_in, cosines, sines):
    half_width = values_in.shape[-1] // 2
    first_half = values_in[..., :half_width]
    second_half = values_in[..., half_width:]
    return jnp.concatenate([first_half * cosines - second_half * sines, second_half * cosines + first_half * sines], -1)

def rms_norm(values_in, gain):
    return values_in * lax.rsqrt(lax.optimization_barrier(jnp.mean(values_in * values_in, -1, keepdims=True)) + EPSILON) * gain

def matmul_hi(left_side, right_side):
    return jnp.dot(left_side, right_side, precision=HIGH)

def silu(values_in):
    return values_in * jax.nn.sigmoid(values_in)

def attend(query, key_nope, key_rope, values):
    qblock = min(512, LEN)
    key_pos = jnp.arange(LEN, dtype=jnp.int32)
    scale = (NOPE + ROPE) ** (-0.5)

    def one_block(block_item):
        query_blk, first_row = block_item
        query_pos = first_row + jnp.arange(qblock, dtype=jnp.int32)
        raw_scores = jnp.einsum('qhd,khd->hqk', query_blk[..., :NOPE], key_nope, precision=HIGH)
        raw_scores = raw_scores + jnp.einsum('qhd,kd->hqk', query_blk[..., NOPE:], key_rope, precision=HIGH)
        raw_scores = low_back(raw_scores)
        allowed = key_pos[None, :] <= query_pos[:, None]
        scores = jnp.where(allowed[None], raw_scores * scale, MASKED)
        row_max = lax.optimization_barrier(jnp.max(scores, -1, keepdims=True))
        exp_terms = jnp.exp(scores - row_max)
        probs_f = exp_terms / lax.optimization_barrier(jnp.sum(exp_terms, -1, keepdims=True))
        mixed_blk = jnp.einsum('hqk,khd->qhd', low(probs_f), values, precision=HIGH)
        return low(low_back(mixed_blk))
    blocks = query.reshape(LEN // qblock, qblock, HEADS, NOPE + ROPE)
    starts = jnp.arange(LEN // qblock, dtype=jnp.int32) * qblock
    mixed_all = lax.map(jax.checkpoint(one_block), (blocks, starts))
    return mixed_all.reshape(LEN, HEADS * VDIM)

def layer_forward(inputs, params, route_mass):
    query_weight, latent_weight, keyval_weight, output_weight, attn_gain, latent_gain, ffn_gain, shared_gate, shared_up, shared_down, expert_gate, expert_up, expert_down = params
    cosines, sines = angles(jnp.arange(LEN, dtype=jnp.int32))
    normed = low(rms_norm(inputs, attn_gain))
    query_raw = low_back(matmul_hi(normed, query_weight)).reshape(LEN, HEADS, NOPE + ROPE)
    query = low(jnp.concatenate([query_raw[..., :NOPE], rotate(query_raw[..., NOPE:], cosines[:, None, :], sines[:, None, :])], -1))
    compressed = low_back(matmul_hi(normed, latent_weight))
    latent = low(rms_norm(compressed[:, :RANK], latent_gain))
    key_rope = low(rotate(compressed[:, RANK:], cosines, sines))
    keyval = low(low_back(matmul_hi(latent, keyval_weight))).reshape(LEN, HEADS, NOPE + VDIM)
    mixed = attend(query, keyval[..., :NOPE], key_rope, keyval[..., NOPE:])
    resid = inputs + low_back(matmul_hi(mixed, output_weight))
    hidden_in = low(rms_norm(resid, ffn_gain))
    gate_s = low_back(matmul_hi(hidden_in, shared_gate))
    up_s = low_back(matmul_hi(hidden_in, shared_up))
    shared_out = matmul_hi(low(silu(gate_s) * up_s), shared_down)

    def expert_step(running, expert_item):
        gate_w, up_w, down_w, expert_mass = expert_item
        rows_in = low_back(hidden_in)
        gate_e = low_back(matmul_hi(rows_in, gate_w))
        up_e = low_back(matmul_hi(rows_in, up_w))
        out_e = low(low_back(matmul_hi(low(silu(gate_e) * up_e), down_w)))
        return (running + expert_mass[:, None] * out_e, None)
    routed, _ = lax.scan(jax.checkpoint(expert_step), jnp.zeros((LEN, D), jnp.float32), (expert_gate, expert_up, expert_down, route_mass.T))
    return resid + shared_out + routed

def reference(layer_input, routes, route_weights, query_weight, latent_weight, keyval_weight, output_weight, attn_gain, latent_gain, ffn_gain, shared_gate, shared_up, shared_down, expert_gate, expert_up, expert_down, cotangent):
    params = tuple((weight.astype(jnp.float32) for weight in (query_weight, latent_weight, keyval_weight, output_weight, attn_gain, latent_gain, ffn_gain, shared_gate, shared_up, shared_down, expert_gate, expert_up, expert_down)))
    inputs = layer_input.astype(jnp.float32).reshape(SEQS, LEN, D)
    grads_in = cotangent.astype(jnp.float32).reshape(SEQS, LEN, D)
    chosen = (routes.reshape(SEQS, LEN, TOPK)[..., None] == jnp.arange(EXPERTS, dtype=jnp.int32)).astype(jnp.float32)
    route_mass = lax.optimization_barrier(jnp.sum(chosen * route_weights.astype(jnp.float32).reshape(SEQS, LEN, TOPK, 1), 2))

    def per_sequence(totals, seq_item):
        seq_in, seq_mass, seq_grad = seq_item

        def forward_fn(values_in, weights):
            return layer_forward(values_in, weights, seq_mass)
        seq_out, pull_back = jax.vjp(forward_fn, seq_in, params)
        d_input, d_params = pull_back(seq_grad)
        totals = jax.tree.map(lambda running, extra: running + extra, totals, d_params)
        return (totals, (seq_out.astype(jnp.bfloat16), d_input))
    zero_grads = jax.tree.map(jnp.zeros_like, params)
    totals, (outputs, input_grads) = lax.scan(per_sequence, zero_grads, (inputs, route_mass, grads_in))
    shape_out = (SEQS, N_CONTEXT, BLOCK, D)
    return (outputs.reshape(shape_out), input_grads.reshape(shape_out), totals[0], totals[1], totals[2], totals[3], totals[4], totals[5], totals[6], totals[7], totals[8], totals[9], totals[10], totals[11], totals[12])
```

```python
import functools

import jax
import jax.numpy as jnp
from jax import lax
from jax.experimental import pallas as pl
from jax.experimental.pallas import tpu as pltpu
from jax.sharding import PartitionSpec as P

D = 2048
NOPE = 128
ROPE = 64
VDIM = 128
RANK = 512
TOPK = 6
EXP_DEV = 2
ROWS = 128
CAPB = 512


EPSILON = 1e-06
ROPE_BASE = 50000.0
MASKED = -1e30


def angles(positions):
    half_width = ROPE // 2
    freqs_table = ROPE_BASE ** (-jnp.arange(half_width, dtype=jnp.float32) * 2.0 / ROPE)
    turned = positions.astype(jnp.float32)[:, None] * freqs_table[None, :]
    return (jnp.cos(turned), jnp.sin(turned))


def rotate(values_in, cosines, sines):
    half_width = values_in.shape[-1] // 2
    first_half = values_in[..., :half_width]
    second_half = values_in[..., half_width:]
    return jnp.concatenate(
        [first_half * cosines - second_half * sines, second_half * cosines + first_half * sines], -1
    )


def rms_scale(values_in):
    return lax.rsqrt(jnp.mean(values_in * values_in, -1, keepdims=True) + EPSILON)


def matmul(left_side, right_side):
    return jnp.dot(left_side, right_side, preferred_element_type=jnp.float32)


def contract_rows(left_side, right_side):
    return lax.dot_general(
        left_side, right_side, (((0,), (0,)), ((), ())), preferred_element_type=jnp.float32
    )


def times_transposed(left_side, right_side):
    return lax.dot_general(
        left_side, right_side, (((1,), (1,)), ((), ())), preferred_element_type=jnp.float32
    )


def silu_parts(gate_vals):
    sigmoid_g = jax.nn.sigmoid(gate_vals)
    return (gate_vals * sigmoid_g, sigmoid_g * (1.0 + gate_vals * (1.0 - sigmoid_g)))


KCHUNK = 512


def attn_fwd_kernel(ctx_ref, q_ref, kn_ref, kr_ref, v_ref, out_ref, lse_ref, *, scale, block_rows):
    q_step = pl.program_id(1)
    rows = q_ref.shape[0]
    query = q_ref[...]

    def step(chunk, carry, masked):
        row_max, denom, acc = carry
        at = pl.ds(pl.multiple_of(chunk * KCHUNK, KCHUNK), KCHUNK)
        keys = jnp.concatenate([kn_ref[at, :], kr_ref[at, :]], -1)
        scores = times_transposed(query, keys) * scale
        if masked:
            row_at = lax.broadcasted_iota(jnp.int32, scores.shape, 0)
            col_at = lax.broadcasted_iota(jnp.int32, scores.shape, 1)
            scores = jnp.where(col_at <= row_at, scores, MASKED)
        new_max = jnp.maximum(row_max, jnp.max(scores, -1, keepdims=True))
        shrink = jnp.exp(row_max - new_max)
        terms = jnp.exp(scores - new_max)
        denom = denom * shrink + jnp.sum(terms, -1, keepdims=True)
        acc = acc * shrink + matmul(terms.astype(jnp.bfloat16), v_ref[at, :])
        return new_max, denom, acc

    carry = (
        jnp.full((rows, 1), MASKED, jnp.float32),
        jnp.zeros((rows, 1), jnp.float32),
        jnp.zeros((rows, VDIM), jnp.float32),
    )
    carry = step(q_step, carry, True)
    carry = lax.fori_loop(0, q_step, lambda i, c: step(i, c, False), carry)
    per_block = block_rows // KCHUNK
    carry = lax.fori_loop(
        per_block, per_block * (1 + ctx_ref[0]), lambda i, c: step(i, c, False), carry
    )
    row_max, denom, acc = carry
    out_ref[...] = (acc / denom).astype(jnp.bfloat16)
    lse_ref[...] = jnp.broadcast_to(row_max + jnp.log(denom), lse_ref.shape)


def attn_forward(my_ctx, query, keyval, key_rope, scale):
    block_rows = query.shape[0]
    seq_len = keyval.shape[0]
    heads = query.shape[1] // 256
    grid_spec = pltpu.PrefetchScalarGridSpec(
        num_scalar_prefetch=1,
        grid=(heads, block_rows // KCHUNK),
        in_specs=[
            pl.BlockSpec((KCHUNK, 256), lambda h, i, c: (i, h)),
            pl.BlockSpec((seq_len, NOPE), lambda h, i, c: (0, 2 * h)),
            pl.BlockSpec((seq_len, 128), lambda h, i, c: (0, 0)),
            pl.BlockSpec((seq_len, VDIM), lambda h, i, c: (0, 2 * h + 1)),
        ],
        out_specs=[
            pl.BlockSpec((KCHUNK, VDIM), lambda h, i, c: (i, h)),
            pl.BlockSpec((KCHUNK, 128), lambda h, i, c: (i, h)),
        ],
    )
    return pl.pallas_call(
        functools.partial(attn_fwd_kernel, scale=scale, block_rows=block_rows),
        grid_spec=grid_spec,
        out_shape=[
            jax.ShapeDtypeStruct((block_rows, heads * VDIM), jnp.bfloat16),
            jax.ShapeDtypeStruct((block_rows, heads * 128), jnp.float32),
        ],
        compiler_params=pltpu.CompilerParams(vmem_limit_bytes=48 * 2**20),
        cost_estimate=pl.CostEstimate(
            flops=4 * 10**9, bytes_accessed=8 * 10**6, transcendentals=2 * 10**6
        ),
        name="attn_forward",
    )(jnp.full((1,), my_ctx, jnp.int32), query, keyval, key_rope, keyval)


def attn_bwd_kernel(
    ctx_ref, q_ref, kn_ref, kr_ref, v_ref, dmix_ref, lse_ref, delta_ref,
    dq_ref, dkv_ref, dkr_ref, dk_acc, dv_acc, *, scale, block_rows,
):
    head = pl.program_id(0)
    q_step = pl.program_id(1)
    rows = q_ref.shape[0]

    @pl.when(q_step == 0)
    def _():
        dv_acc[...] = jnp.zeros_like(dv_acc)
        dk_acc[:, :NOPE] = jnp.zeros((dk_acc.shape[0], NOPE), jnp.float32)

    @pl.when((q_step == 0) & (head == 0))
    def _():
        dk_acc[:, NOPE:] = jnp.zeros((dk_acc.shape[0], 128), jnp.float32)

    query = q_ref[...]
    dmix = dmix_ref[...]
    lse = lse_ref[0]
    delta = delta_ref[0]

    def step(chunk, d_query, masked):
        at = pl.ds(pl.multiple_of(chunk * KCHUNK, KCHUNK), KCHUNK)
        keys = jnp.concatenate([kn_ref[at, :], kr_ref[at, :]], -1)
        scores = times_transposed(keys, query) * scale - lse
        if masked:
            key_at = lax.broadcasted_iota(jnp.int32, scores.shape, 0)
            row_at = lax.broadcasted_iota(jnp.int32, scores.shape, 1)
            scores = jnp.where(key_at <= row_at, scores, MASKED)
        probs = jnp.exp(scores)
        dprob = times_transposed(v_ref[at, :], dmix)
        d_raw = (probs * (dprob - delta) * scale).astype(jnp.bfloat16)
        dv_acc[at, :] += matmul(probs.astype(jnp.bfloat16), dmix)
        dk_acc[at, :] += matmul(d_raw, query)
        return d_query + contract_rows(d_raw, keys)

    d_query = step(q_step, jnp.zeros((rows, 256), jnp.float32), True)
    d_query = lax.fori_loop(0, q_step, lambda i, c: step(i, c, False), d_query)
    per_block = block_rows // KCHUNK
    d_query = lax.fori_loop(
        per_block, per_block * (1 + ctx_ref[0]), lambda i, c: step(i, c, False), d_query
    )
    dq_ref[...] = d_query

    @pl.when(q_step == pl.num_programs(1) - 1)
    def _():
        dkv_ref[:, :NOPE] = dk_acc[:, :NOPE].astype(jnp.bfloat16)
        dkv_ref[:, NOPE:] = dv_acc[...].astype(jnp.bfloat16)

    @pl.when((q_step == pl.num_programs(1) - 1) & (head == pl.num_programs(0) - 1))
    def _():
        dkr_ref[...] = dk_acc[:, NOPE:].astype(jnp.bfloat16)


def attn_backward(my_ctx, query, keyval, key_rope, d_mixed, lse_rows, delta_rows, scale):
    block_rows = query.shape[0]
    seq_len = keyval.shape[0]
    heads = query.shape[1] // 256
    grid_spec = pltpu.PrefetchScalarGridSpec(
        num_scalar_prefetch=1,
        grid=(heads, block_rows // KCHUNK),
        in_specs=[
            pl.BlockSpec((KCHUNK, 256), lambda h, i, c: (i, h)),
            pl.BlockSpec((seq_len, NOPE), lambda h, i, c: (0, 2 * h)),
            pl.BlockSpec((seq_len, 128), lambda h, i, c: (0, 0)),
            pl.BlockSpec((seq_len, VDIM), lambda h, i, c: (0, 2 * h + 1)),
            pl.BlockSpec((KCHUNK, VDIM), lambda h, i, c: (i, h)),
            pl.BlockSpec((1, 1, KCHUNK), lambda h, i, c: (h, 0, i)),
            pl.BlockSpec((1, 1, KCHUNK), lambda h, i, c: (h, 0, i)),
        ],
        out_specs=[
            pl.BlockSpec((KCHUNK, 256), lambda h, i, c: (i, h)),
            pl.BlockSpec((seq_len, 256), lambda h, i, c: (0, h)),
            pl.BlockSpec((seq_len, 128), lambda h, i, c: (0, 0)),
        ],
        scratch_shapes=[
            pltpu.VMEM((seq_len, 256), jnp.float32),
            pltpu.VMEM((seq_len, VDIM), jnp.float32),
        ],
    )
    return pl.pallas_call(
        functools.partial(attn_bwd_kernel, scale=scale, block_rows=block_rows),
        grid_spec=grid_spec,
        out_shape=[
            jax.ShapeDtypeStruct((block_rows, heads * 256), jnp.float32),
            jax.ShapeDtypeStruct((seq_len, heads * 256), jnp.bfloat16),
            jax.ShapeDtypeStruct((seq_len, 128), jnp.bfloat16),
        ],
        compiler_params=pltpu.CompilerParams(vmem_limit_bytes=56 * 2**20),
        cost_estimate=pl.CostEstimate(
            flops=10 * 10**9, bytes_accessed=10 * 10**6, transcendentals=4 * 10**6
        ),
        name="attn_backward",
    )(
        jnp.full((1,), my_ctx, jnp.int32),
        query, keyval, key_rope, keyval, d_mixed, lse_rows, delta_rows,
    )


def turn(values, axis, step):
    size = lax.axis_size(axis)
    return lax.ppermute(values, axis, [(i, (i + step) % size) for i in range(size)])


def move(values, step, cross):
    n_exp = lax.axis_size("experts")
    half = n_exp // 2
    pairs = [
        (i, ((i // 2 + step) % half) * 2 + ((i % 2) ^ cross)) for i in range(n_exp)
    ]
    return lax.ppermute(values, "experts", pairs)


def places():
    n_exp = lax.axis_size("experts")
    half = n_exp // 2
    mine = lax.axis_index("experts")
    found = []
    for step in range(half):
        for cross in range(2):
            pair = (mine % 2) ^ cross if cross else mine % 2
            target = ((mine // 2 + step) % half) * 2 + pair
            source = ((mine // 2 + half - step) % half) * 2 + pair
            found.append((step, cross, target, source))
    return found


def gather_slots(values):
    half = lax.axis_size("experts") // 2
    slots = []
    for step in range(half):
        here = move(values, step, 0) if step else values
        slots += [here, move(here, 0, 1)]
    return slots


def scatter_sum(part_of):
    half = lax.axis_size("experts") // 2
    where = places()
    total = None
    for step in list(range(1, half)) + [0]:
        near, far = where[2 * step][2], where[2 * step + 1][2]
        pair = part_of(near).astype(jnp.float32) + move(part_of(far), 0, 1).astype(jnp.float32)
        if step:
            pair = move(pair.astype(jnp.bfloat16), step, 0).astype(jnp.float32)
        total = pair if total is None else total + pair
    return total


def swap_all(part_of):
    got = []
    for step, cross, target, source in places():
        part = part_of(target)
        got.append((source, move(part, step, cross) if step or cross else part))
    return got


def butterfly(values, axis):
    size = lax.axis_size(axis)
    span = 1
    while span < size:
        pairs = [(i, i ^ span) for i in range(size)]
        values = values + lax.ppermute(values, axis, pairs)
        span *= 2
    return values


def gather_quarters(shard, dim):
    n_ctx, n_dp = lax.axis_size("context"), lax.axis_size("dp")
    my_ctx, my_dp = lax.axis_index("context"), lax.axis_index("dp")
    width = shard.shape[dim]
    shape = list(shard.shape)
    shape[dim] = width * n_ctx * n_dp
    whole = jnp.zeros(shape, shard.dtype)
    for k in range(n_ctx):
        row = turn(shard, "context", k) if k else shard
        for j in range(n_dp):
            piece = turn(row, "dp", j) if j else row
            at = (my_ctx + n_ctx - k) % n_ctx * n_dp + (my_dp + n_dp - j) % n_dp
            whole = lax.dynamic_update_slice_in_dim(whole, piece, at * width, dim)
    return whole


def scatter_quarters(part_of):
    n_ctx, n_dp = lax.axis_size("context"), lax.axis_size("dp")
    my_ctx, my_dp = lax.axis_index("context"), lax.axis_index("dp")
    total = None
    for k in list(range(1, n_ctx)) + [0]:
        ctx_at = (my_ctx + k) % n_ctx
        near = None
        for j in list(range(1, n_dp)) + [0]:
            part = part_of(ctx_at, (my_dp + j) % n_dp)
            if j:
                part = turn(part.astype(jnp.bfloat16), "dp", j).astype(jnp.float32)
            near = part if near is None else near + part
        if k:
            near = turn(near.astype(jnp.bfloat16), "context", k).astype(jnp.float32)
        total = near if total is None else total + near
    return total


def sum_weight_grad(grad):
    n_ctx, n_dp = lax.axis_size("context"), lax.axis_size("dp")
    my_dp = lax.axis_index("dp")
    rows = grad.shape[0] // n_dp
    part = lambda j: lax.dynamic_slice_in_dim(grad, (my_dp + j) % n_dp * rows, rows, 0)
    own = part(0)
    for j in range(1, n_dp):
        own = own + turn(part(j).astype(jnp.bfloat16), "dp", j).astype(jnp.float32)
    own = own.astype(jnp.bfloat16)
    if n_ctx == 2:
        own = own.astype(jnp.float32) + turn(own, "context", 1).astype(jnp.float32)
        own = own.astype(jnp.bfloat16)
    else:
        own = lax.psum(own, "context")
    whole = jnp.zeros(grad.shape, jnp.bfloat16)
    for j in range(n_dp):
        piece = turn(own, "dp", j) if j else own
        at = (my_dp + n_dp - j) % n_dp
        whole = lax.dynamic_update_slice_in_dim(whole, piece, at * rows, 0)
    return whole.astype(jnp.float32)


def local(
    layer_input,
    routes,
    route_weights,
    query_weight,
    latent_weight,
    keyval_weight,
    output_weight,
    attn_gain,
    latent_gain,
    ffn_gain,
    shared_gate,
    shared_up,
    shared_down,
    expert_gate,
    expert_up,
    expert_down,
    cotangent,
):
    n_exp = lax.axis_size("experts")
    n_ctx = lax.axis_size("context")
    n_dp = lax.axis_size("dp")
    my_exp = lax.axis_index("experts")
    my_ctx = lax.axis_index("context")
    my_dp = lax.axis_index("dp")
    block_rows = layer_input.shape[2]
    heads_dev = query_weight.shape[1] // (NOPE + ROPE)
    scale = (NOPE + ROPE) ** (-0.5)
    low = jnp.bfloat16
    inputs = layer_input.reshape(block_rows, D).astype(jnp.float32)
    route_ids = routes.reshape(block_rows, TOPK)
    route_mass = route_weights.reshape(block_rows, TOPK)
    grad_out = cotangent.reshape(block_rows, D)
    own_start = my_exp * ROWS

    def own_rows(values):
        return lax.dynamic_slice_in_dim(values, own_start, ROWS, 0)

    full_gate = gather_quarters(expert_gate, 1)
    full_up = gather_quarters(expert_up, 1)
    full_down = gather_quarters(expert_down, 2)
    ow_rows = output_weight.shape[0] // n_dp
    ow_part = lax.dynamic_slice_in_dim(output_weight, my_dp * ow_rows, ow_rows, 0)
    ow_near = jnp.concatenate(gather_slots(ow_part), 0)
    ow_full = jnp.concatenate([ow_near] + [turn(ow_near, "dp", j) for j in range(1, n_dp)], 0)

    query_pos = my_ctx * block_rows + jnp.arange(block_rows, dtype=jnp.int32)
    cos_q, sin_q = angles(query_pos)
    normed = (inputs * rms_scale(inputs) * attn_gain).astype(low)
    compressed = matmul(normed, latent_weight)

    def latent_fn(comp_rows, lat_gain, cosines, sines):
        lat_part = comp_rows[:, :RANK] * rms_scale(comp_rows[:, :RANK]) * lat_gain
        return jnp.concatenate([lat_part, rotate(comp_rows[:, RANK:], cosines, sines)], -1)

    kv_low = latent_fn(compressed, latent_gain, cos_q, sin_q).astype(low)
    kv_blocks = [kv_low]
    for k in range(1, n_ctx):
        pairs = [(i, i + k) for i in range(n_ctx - k)]
        kv_blocks.append(lax.ppermute(kv_low, "context", pairs))
    kv_all = jnp.concatenate(kv_blocks, 0)
    latent_all = kv_all[:, :RANK]
    key_rope = jnp.pad(kv_all[:, RANK:], ((0, 0), (0, 128 - ROPE)))
    expanded = matmul(latent_all, keyval_weight).astype(low)
    query_raw = matmul(normed, query_weight).reshape(block_rows, heads_dev, NOPE + ROPE)
    query = jnp.concatenate(
        [
            query_raw[..., :NOPE],
            rotate(query_raw[..., NOPE:], cos_q[:, None, :], sin_q[:, None, :]),
            jnp.zeros((block_rows, heads_dev, 256 - NOPE - ROPE), jnp.float32),
        ],
        -1,
    ).astype(low).reshape(block_rows, heads_dev * 256)
    mixed, logsums = attn_forward(my_ctx, query, expanded, key_rope, scale)

    def head_turn(values, back):
        step = my_dp * VDIM * (heads_dev // n_dp)
        width = values.shape[1]
        twice = jnp.concatenate([values, values], 1)
        start = (width - step) % width if back else step
        return lax.dynamic_slice_in_dim(twice, start, width, 1)

    mixed_slots = gather_slots(head_turn(mixed, False))
    mixed_full = jnp.concatenate(
        [s[:, j * ow_rows : (j + 1) * ow_rows] for j in range(n_dp) for s in mixed_slots], 1
    )
    resid = inputs + matmul(mixed_full, ow_full)
    scale_mid = rms_scale(resid)
    hidden_in = (resid * scale_mid * ffn_gain).astype(low)
    resid_own = own_rows(resid)
    scale_mid_own = own_rows(scale_mid)

    expert_ids = my_exp * EXP_DEV + jnp.arange(EXP_DEV, dtype=jnp.int32)
    chosen = route_ids[:, :, None] == expert_ids[None, None, :]
    member = jnp.any(chosen, 1)
    mass = jnp.sum(jnp.where(chosen, route_mass[:, :, None], 0.0), 1)
    earlier = (
        jnp.arange(block_rows, dtype=jnp.int32)[:, None]
        > jnp.arange(block_rows, dtype=jnp.int32)[None, :]
    ).astype(low)
    rank = matmul(earlier, member.astype(low)).astype(jnp.int32)
    slot_of = jnp.where(member, rank, -1).T
    taken = slot_of[:, None, :] == jnp.arange(CAPB, dtype=jnp.int32)[None, :, None]
    slot_mass = jnp.sum(jnp.where(taken, mass.T[:, None, :], 0.0), -1)
    pick = taken.astype(low).reshape(EXP_DEV * CAPB, block_rows)

    d_out = (
        (matmul(pick, grad_out) * slot_mass.reshape(-1, 1)).astype(low).reshape(EXP_DEV, CAPB, D)
    )
    expert_in = matmul(pick, hidden_in).astype(low).reshape(EXP_DEV, CAPB, D)
    gate_e = jnp.einsum("ecd,edf->ecf", expert_in, full_gate, preferred_element_type=jnp.float32)
    up_e = jnp.einsum("ecd,edf->ecf", expert_in, full_up, preferred_element_type=jnp.float32)
    silu_e, slope_e = silu_parts(gate_e)
    act_e = (silu_e * up_e).astype(low)
    quarter = D // (n_ctx * n_dp)

    def columns(values, ctx_at, dp_at):
        return lax.dynamic_slice_in_dim(values, (ctx_at * n_dp + dp_at) * quarter, quarter, 2)

    expert_down_grad = scatter_quarters(
        lambda c, d: jnp.einsum(
            "ecf,ecd->efd", act_e, columns(d_out, c, d), preferred_element_type=jnp.float32
        )
    )
    d_act_e = jnp.einsum("ecd,efd->ecf", d_out, full_down, preferred_element_type=jnp.float32)
    d_up_e = (d_act_e * silu_e).astype(low)
    d_gate_e = (d_act_e * up_e * slope_e).astype(low)
    expert_gate_grad = scatter_quarters(
        lambda c, d: jnp.einsum(
            "ecd,ecf->edf", columns(expert_in, c, d), d_gate_e, preferred_element_type=jnp.float32
        )
    )
    expert_up_grad = scatter_quarters(
        lambda c, d: jnp.einsum(
            "ecd,ecf->edf", columns(expert_in, c, d), d_up_e, preferred_element_type=jnp.float32
        )
    )
    d_in_e = (
        jnp.einsum("ecf,edf->ecd", d_gate_e, full_gate, preferred_element_type=jnp.float32)
        + jnp.einsum("ecf,edf->ecd", d_up_e, full_up, preferred_element_type=jnp.float32)
    ).astype(low)
    out_e = jnp.einsum("ecf,efd->ecd", act_e, full_down, preferred_element_type=jnp.float32)
    out_e = (out_e * slot_mass[:, :, None]).astype(low)

    gate_s = matmul(hidden_in, shared_gate)
    up_s = matmul(hidden_in, shared_up)
    silu_s, slope_s = silu_parts(gate_s)
    act_s = (silu_s * up_s).astype(low)
    d_act_s = times_transposed(grad_out, shared_down)
    d_up_s = (d_act_s * silu_s).astype(low)
    d_gate_s = (d_act_s * up_s * slope_s).astype(low)
    d_hidden_part = (
        times_transposed(d_gate_s, shared_gate)
        + times_transposed(d_up_s, shared_up)
        + contract_rows(pick, d_in_e.reshape(EXP_DEV * CAPB, D))
    ).astype(low)

    def row_part(values):
        return lambda target: lax.dynamic_slice_in_dim(values, target * ROWS, ROWS, 0)

    d_hidden_own = scatter_sum(row_part(d_hidden_part))
    grad_own = own_rows(grad_out).astype(jnp.float32)

    def norm_mid(values_in):
        return values_in * rms_scale(values_in) * ffn_gain

    _, mid_pull = jax.vjp(norm_mid, resid_own)
    d_resid_own = grad_own + mid_pull(d_hidden_own)[0]
    d_ffn_gain = jnp.sum(d_hidden_own * resid_own * scale_mid_own, 0)
    d_resid_low = d_resid_own.astype(low)
    d_mixed_slots = times_transposed(d_resid_low, ow_full).astype(low)

    half = n_exp // 2

    def to_source(step, cross, k):
        parts = [
            d_mixed_slots[:, (j * n_exp + k) * ow_rows : (j * n_exp + k + 1) * ow_rows]
            for j in range(n_dp)
        ]
        part = jnp.concatenate(parts, 1)
        return move(part, (half - step) % half, cross) if step or cross else part

    d_mixed_turned = jnp.zeros((block_rows, heads_dev * VDIM), low)
    for k, (step, cross, target, source) in enumerate(places()):
        d_mixed_turned = lax.dynamic_update_slice_in_dim(
            d_mixed_turned, to_source(step, cross, k), target * ROWS, 0
        )
    d_mixed = head_turn(d_mixed_turned, True)

    delta = jnp.sum(
        (d_mixed.astype(jnp.float32) * mixed.astype(jnp.float32)).reshape(
            block_rows, heads_dev, VDIM
        ),
        -1,
    )
    delta_rows = delta.T.reshape(heads_dev, 1, block_rows)
    lse_rows = logsums[:, ::128].T.reshape(heads_dev, 1, block_rows)
    d_query, d_kv, d_krope = attn_backward(
        my_ctx, query, expanded, key_rope, d_mixed, lse_rows, delta_rows, scale
    )
    d_latent_part = jnp.concatenate(
        [times_transposed(d_kv, keyval_weight).astype(low), d_krope[:, :ROPE]], -1
    ).reshape(n_ctx, block_rows, RANK + ROPE)
    d_lat_blocks = scatter_sum(
        lambda target: lax.dynamic_slice_in_dim(d_latent_part, target * ROWS, ROWS, 1)
    )
    d_comp_own = d_lat_blocks[0]
    for k in range(1, n_ctx):
        pairs = [(i, i - k) for i in range(k, n_ctx)]
        d_comp_own = d_comp_own + lax.ppermute(
            d_lat_blocks[k].astype(low), "context", pairs
        ).astype(jnp.float32)
    d_query = d_query.reshape(block_rows, heads_dev, 256)
    d_query_low = (
        jnp.concatenate(
            [
                d_query[..., :NOPE],
                rotate(
                    d_query[..., NOPE : NOPE + ROPE], cos_q[:, None, :], -sin_q[:, None, :]
                ),
            ],
            -1,
        )
        .astype(low)
        .reshape(block_rows, heads_dev * (NOPE + ROPE))
    )
    half_rows = D // n_dp
    qw_part = lax.dynamic_slice_in_dim(query_weight, my_dp * half_rows, half_rows, 0)
    qw_part, _ = lax.optimization_barrier((qw_part, hidden_in))
    qw_near = jnp.concatenate(gather_slots(qw_part), 1)
    qw_parts = [qw_near] + [turn(qw_near, "dp", j) for j in range(1, n_dp)]
    dq_own = jnp.concatenate([part for _, part in swap_all(row_part(d_query_low))], 1)
    d_norm_own = jnp.zeros((ROWS, D), jnp.float32)
    for j in range(n_dp):
        at = (my_dp + n_dp - j) % n_dp
        d_norm_own = lax.dynamic_update_slice_in_dim(
            d_norm_own, times_transposed(dq_own, qw_parts[j]), at * half_rows, 1
        )

    own_pos = my_ctx * block_rows + own_start + jnp.arange(ROWS, dtype=jnp.int32)
    cos_k, sin_k = angles(own_pos)
    _, kv_pull = jax.vjp(
        lambda c, g: latent_fn(c, g, cos_k, sin_k), own_rows(compressed), latent_gain
    )
    d_comp, d_lat_gain = kv_pull(d_comp_own)
    d_comp_low = d_comp.astype(low)
    own_normed = own_rows(normed)
    d_norm_total = d_norm_own + times_transposed(d_comp_low, latent_weight)

    def norm_in(values_in, gain_in):
        return values_in * rms_scale(values_in) * gain_in

    _, in_pull = jax.vjp(norm_in, own_rows(inputs), attn_gain)
    d_in_rows, d_attn_gain = in_pull(d_norm_total)
    input_grad = (d_resid_own + d_in_rows).reshape(1, 1, ROWS, D)

    ffn_part = (
        matmul(act_s, shared_down)
        + contract_rows(pick, out_e.reshape(EXP_DEV * CAPB, D))
    ).astype(low)
    ffn_out = scatter_sum(row_part(ffn_part))
    layer_output = (resid_own + ffn_out).astype(low).reshape(1, 1, ROWS, D)

    shared_gate_grad = sum_weight_grad(contract_rows(hidden_in, d_gate_s))
    shared_up_grad = sum_weight_grad(contract_rows(hidden_in, d_up_s))
    shared_down_grad = sum_weight_grad(contract_rows(act_s, grad_out))
    query_grad = sum_weight_grad(contract_rows(normed, d_query_low))
    keyval_grad = sum_weight_grad(contract_rows(latent_all, d_kv))
    d_resid_block = jnp.zeros((block_rows, D), low)
    for (_, _, _, source), rows in zip(places(), gather_slots(d_resid_low)):
        d_resid_block = lax.dynamic_update_slice_in_dim(d_resid_block, rows, source * ROWS, 0)
    output_grad = sum_weight_grad(contract_rows(mixed, d_resid_block))

    grad_latent = contract_rows(own_normed, d_comp_low)
    lat_cols = grad_latent.shape[0] // n_dp
    lat_rows = lat_cols // n_exp
    part = lambda j: lax.dynamic_slice_in_dim(
        grad_latent, (my_dp + j) % n_dp * lat_cols, lat_cols, 0
    )
    lat_half = part(0)
    for j in range(1, n_dp):
        lat_half = lat_half + turn(part(j).astype(low), "dp", j).astype(jnp.float32)
    lat_half = lat_half.astype(low)
    lat_own = scatter_sum(
        lambda target: lax.dynamic_slice_in_dim(lat_half, target * lat_rows, lat_rows, 0)
    )
    lat_own = butterfly(lat_own, "context").astype(low)
    lat_half = jnp.zeros((lat_cols, RANK + ROPE), low)
    for (_, _, _, source), rows in zip(places(), gather_slots(lat_own)):
        lat_half = lax.dynamic_update_slice_in_dim(lat_half, rows, source * lat_rows, 0)
    latent_grad = jnp.zeros(grad_latent.shape, low)
    for j in range(n_dp):
        piece = turn(lat_half, "dp", j) if j else lat_half
        at = (my_dp + n_dp - j) % n_dp
        latent_grad = lax.dynamic_update_slice_in_dim(latent_grad, piece, at * lat_cols, 0)
    latent_grad = latent_grad.astype(jnp.float32)

    gains = jnp.concatenate([d_attn_gain, d_lat_gain, d_ffn_gain])
    for axis in ("dp", "context", "experts"):
        gains = butterfly(gains, axis)
    attn_gain_grad = gains[:D]
    latent_gain_grad = gains[D : D + RANK]
    ffn_gain_grad = gains[D + RANK :]
    return (
        layer_output,
        input_grad,
        query_grad,
        latent_grad,
        keyval_grad,
        output_grad,
        attn_gain_grad,
        latent_gain_grad,
        ffn_gain_grad,
        shared_gate_grad,
        shared_up_grad,
        shared_down_grad,
        expert_gate_grad,
        expert_up_grad,
        expert_down_grad,
    )


def solution(mesh):
    in_specs = (
        P("dp", "context", None, None),
        P("dp", "context", None, None),
        P("dp", "context", None, None),
        P(None, "experts"),
        P(),
        P(None, "experts"),
        P("experts", None),
        P(),
        P(),
        P(),
        P(None, "experts"),
        P(None, "experts"),
        P("experts", None),
        P("experts", ("context", "dp"), None),
        P("experts", ("context", "dp"), None),
        P("experts", None, ("context", "dp")),
        P("dp", "context", None, None),
    )
    out_specs = (
        P("dp", "context", "experts", None),
        P("dp", "context", "experts", None),
        P(None, "experts"),
        P(),
        P(None, "experts"),
        P("experts", None),
        P(),
        P(),
        P(),
        P(None, "experts"),
        P(None, "experts"),
        P("experts", None),
        P("experts", ("context", "dp"), None),
        P("experts", ("context", "dp"), None),
        P("experts", None, ("context", "dp")),
    )
    return jax.shard_map(local, mesh=mesh, in_specs=in_specs, out_specs=out_specs, check_vma=False)
```

```python
import functools

import jax
import jax.numpy as jnp
from jax import lax
from jax.experimental import pallas as pl
from jax.experimental.pallas import tpu as pltpu
from jax.sharding import PartitionSpec as P

D = 2048
NOPE = 128
ROPE = 64
VDIM = 128
RANK = 512
TOPK = 6
EXP_DEV = 2
ROWS = 128
CAPB = 512


EPSILON = 1e-06
ROPE_BASE = 50000.0
MASKED = -1e30


def angles(positions):
    half_width = ROPE // 2
    freqs_table = ROPE_BASE ** (-jnp.arange(half_width, dtype=jnp.float32) * 2.0 / ROPE)
    turned = positions.astype(jnp.float32)[:, None] * freqs_table[None, :]
    return (jnp.cos(turned), jnp.sin(turned))


def rotate(values_in, cosines, sines):
    half_width = values_in.shape[-1] // 2
    first_half = values_in[..., :half_width]
    second_half = values_in[..., half_width:]
    return jnp.concatenate(
        [first_half * cosines - second_half * sines, second_half * cosines + first_half * sines], -1
    )


def rms_scale(values_in):
    return lax.rsqrt(jnp.mean(values_in * values_in, -1, keepdims=True) + EPSILON)


def matmul(left_side, right_side):
    return jnp.dot(left_side, right_side, preferred_element_type=jnp.float32)


def contract_rows(left_side, right_side):
    return lax.dot_general(
        left_side, right_side, (((0,), (0,)), ((), ())), preferred_element_type=jnp.float32
    )


def times_transposed(left_side, right_side):
    return lax.dot_general(
        left_side, right_side, (((1,), (1,)), ((), ())), preferred_element_type=jnp.float32
    )


def silu_parts(gate_vals):
    sigmoid_g = jax.nn.sigmoid(gate_vals)
    return (gate_vals * sigmoid_g, sigmoid_g * (1.0 + gate_vals * (1.0 - sigmoid_g)))


KCHUNK = 512
VMEM_LIMIT = 56 * 2**20


def params():
    return pltpu.CompilerParams(vmem_limit_bytes=VMEM_LIMIT)


def cost(gflop, mbytes):
    return pl.CostEstimate(
        flops=int(gflop * 1e9), bytes_accessed=int(mbytes * 1e6), transcendentals=0
    )


def whole(shape):
    zeros = (0,) * len(shape)
    return pl.BlockSpec(shape, lambda *at: zeros)


def turned(tile, cosines, sines):
    lane = lax.broadcasted_iota(jnp.int32, tile.shape, 1)
    half_width = ROPE // 2
    other = jnp.where(
        lane < half_width, pltpu.roll(tile, 128 - half_width, 1), pltpu.roll(tile, half_width, 1)
    )
    return tile * cosines + other * sines


def front_kernel(x_ref, gain_ref, wq_ref, wl_ref, lgain_ref, cos_ref, sin_ref, normed_ref, q_ref, kv_ref):
    x = x_ref[...].astype(jnp.float32)
    normed = (x * rms_scale(x) * gain_ref[...]).astype(jnp.bfloat16)
    normed_ref[...] = normed
    cosines, sines = cos_ref[...], sin_ref[...]
    low_part = times_transposed(normed, wl_ref[:RANK, :])
    kv_ref[:, :RANK] = (low_part * rms_scale(low_part) * lgain_ref[...]).astype(jnp.bfloat16)
    rope_rows = jnp.concatenate([wl_ref[RANK:, :], jnp.zeros((128 - ROPE, D), jnp.bfloat16)], 0)
    rope_part = times_transposed(normed, rope_rows)
    kv_ref[:, RANK:] = turned(rope_part, cosines, sines).astype(jnp.bfloat16)
    raw = matmul(normed, wq_ref[...])
    width = raw.shape[1]
    for head in range(width // (NOPE + ROPE)):
        start = head * (NOPE + ROPE)
        here = pltpu.roll(raw, width - start, 1) if start else raw
        q_ref[:, head * 256 : head * 256 + NOPE] = here[:, :NOPE].astype(jnp.bfloat16)
        q_ref[:, head * 256 + NOPE : head * 256 + 256] = turned(
            here[:, NOPE : NOPE + 128], cosines, sines
        ).astype(jnp.bfloat16)


def front(x, gain, query_weight, latent_turned, lat_gain, cosines, sines):
    rows = x.shape[0]
    blk = 512
    heads = query_weight.shape[1] // (NOPE + ROPE)
    row_spec = lambda width: pl.BlockSpec((blk, width), lambda i: (i, 0))
    return pl.pallas_call(
        front_kernel,
        grid=(rows // blk,),
        in_specs=[
            row_spec(D), whole((1, D)), whole(query_weight.shape), whole(latent_turned.shape),
            whole((1, RANK)), row_spec(128), row_spec(128),
        ],
        out_specs=[row_spec(D), row_spec(heads * 256), row_spec(RANK + 128)],
        out_shape=[
            jax.ShapeDtypeStruct((rows, D), jnp.bfloat16),
            jax.ShapeDtypeStruct((rows, heads * 256), jnp.bfloat16),
            jax.ShapeDtypeStruct((rows, RANK + 128), jnp.bfloat16),
        ],
        compiler_params=params(),
        cost_estimate=cost(4.5, 16),
        name="front",
    )(x, gain.reshape(1, D), query_weight, latent_turned, lat_gain.reshape(1, RANK), cosines, sines)


def to_row(column_tile):
    ones = jnp.ones((8, 128), jnp.float32)
    return lax.dot_general(
        ones, column_tile, (((1,), (1,)), ((), ())),
        precision=lax.Precision.HIGHEST, preferred_element_type=jnp.float32,
    )[0:1]


def attn_fwd_kernel(ctx_ref, q_ref, kn_ref, kr_ref, v_ref, out_ref, lse_ref, *, scale, block_rows):
    q_step = pl.program_id(1)
    rows = q_ref.shape[0]
    query = q_ref[...]

    def step(chunk, carry, masked):
        row_max, denom, acc = carry
        at = pl.ds(pl.multiple_of(chunk * KCHUNK, KCHUNK), KCHUNK)
        keys = jnp.concatenate([kn_ref[at, :], kr_ref[at, :]], -1)
        scores = times_transposed(query, keys) * scale
        if masked:
            row_at = lax.broadcasted_iota(jnp.int32, scores.shape, 0)
            col_at = lax.broadcasted_iota(jnp.int32, scores.shape, 1)
            scores = jnp.where(col_at <= row_at, scores, MASKED)
        new_max = jnp.maximum(row_max, jnp.max(scores, -1, keepdims=True))
        shrink = jnp.exp(row_max - new_max)
        terms = jnp.exp(scores - new_max)
        denom = denom * shrink + jnp.sum(terms, -1, keepdims=True)
        acc = acc * shrink + matmul(terms.astype(jnp.bfloat16), v_ref[at, :])
        return new_max, denom, acc

    carry = (
        jnp.full((rows, 1), MASKED, jnp.float32),
        jnp.zeros((rows, 1), jnp.float32),
        jnp.zeros((rows, VDIM), jnp.float32),
    )
    carry = step(q_step, carry, True)
    carry = lax.fori_loop(0, q_step, lambda i, c: step(i, c, False), carry)
    per_block = block_rows // KCHUNK
    carry = lax.fori_loop(
        per_block, per_block * (1 + ctx_ref[0]), lambda i, c: step(i, c, False), carry
    )
    row_max, denom, acc = carry
    out_ref[...] = (acc / denom).astype(jnp.bfloat16)
    lane = lax.broadcasted_iota(jnp.int32, (rows, 128), 1)
    lse_ref[0] = to_row(jnp.where(lane == 0, row_max + jnp.log(denom), 0.0))


def attn_forward(my_ctx, query, keyval, kv_all, scale):
    block_rows = query.shape[0]
    seq_len = keyval.shape[0]
    heads = query.shape[1] // 256
    grid_spec = pltpu.PrefetchScalarGridSpec(
        num_scalar_prefetch=1,
        grid=(heads, block_rows // KCHUNK),
        in_specs=[
            pl.BlockSpec((KCHUNK, 256), lambda h, i, c: (i, h)),
            pl.BlockSpec((seq_len, NOPE), lambda h, i, c: (0, 2 * h)),
            pl.BlockSpec((seq_len, 128), lambda h, i, c: (0, RANK // 128)),
            pl.BlockSpec((seq_len, VDIM), lambda h, i, c: (0, 2 * h + 1)),
        ],
        out_specs=[
            pl.BlockSpec((KCHUNK, VDIM), lambda h, i, c: (i, h)),
            pl.BlockSpec((1, 1, KCHUNK), lambda h, i, c: (h, 0, i)),
        ],
    )
    return pl.pallas_call(
        functools.partial(attn_fwd_kernel, scale=scale, block_rows=block_rows),
        grid_spec=grid_spec,
        out_shape=[
            jax.ShapeDtypeStruct((block_rows, heads * VDIM), jnp.bfloat16),
            jax.ShapeDtypeStruct((heads, 1, block_rows), jnp.float32),
        ],
        compiler_params=params(),
        cost_estimate=cost(4, 8),
        name="attn_forward",
    )(jnp.full((1,), my_ctx, jnp.int32), query, keyval, kv_all, keyval)


def attn_bwd_kernel(
    ctx_ref, q_ref, kn_ref, kr_ref, v_ref, dmix_ref, mix_ref, lse_ref, cos_ref, sin_ref,
    dq_ref, dkv_ref, dkr_ref, dk_acc, dv_acc, *, scale, block_rows,
):
    head = pl.program_id(0)
    q_step = pl.program_id(1)
    rows = q_ref.shape[0]

    @pl.when(q_step == 0)
    def _():
        dv_acc[...] = jnp.zeros_like(dv_acc)
        dk_acc[:, :NOPE] = jnp.zeros((dk_acc.shape[0], NOPE), jnp.float32)

    @pl.when((q_step == 0) & (head == 0))
    def _():
        dk_acc[:, NOPE:] = jnp.zeros((dk_acc.shape[0], 128), jnp.float32)

    query = q_ref[...]
    dmix = dmix_ref[...]
    lse = lse_ref[0]
    delta = to_row(dmix.astype(jnp.float32) * mix_ref[...].astype(jnp.float32))

    def step(chunk, d_query, masked):
        at = pl.ds(pl.multiple_of(chunk * KCHUNK, KCHUNK), KCHUNK)
        keys = jnp.concatenate([kn_ref[at, :], kr_ref[at, :]], -1)
        scores = times_transposed(keys, query) * scale - lse
        if masked:
            key_at = lax.broadcasted_iota(jnp.int32, scores.shape, 0)
            row_at = lax.broadcasted_iota(jnp.int32, scores.shape, 1)
            scores = jnp.where(key_at <= row_at, scores, MASKED)
        probs = jnp.exp(scores)
        dprob = times_transposed(v_ref[at, :], dmix)
        d_raw = (probs * (dprob - delta) * scale).astype(jnp.bfloat16)
        dv_acc[at, :] += matmul(probs.astype(jnp.bfloat16), dmix)
        dk_acc[at, :] += matmul(d_raw, query)
        return d_query + contract_rows(d_raw, keys)

    d_query = step(q_step, jnp.zeros((rows, 256), jnp.float32), True)
    d_query = lax.fori_loop(0, q_step, lambda i, c: step(i, c, False), d_query)
    per_block = block_rows // KCHUNK
    d_query = lax.fori_loop(
        per_block, per_block * (1 + ctx_ref[0]), lambda i, c: step(i, c, False), d_query
    )
    dq_ref[:, :NOPE] = d_query[:, :NOPE].astype(jnp.bfloat16)
    dq_ref[:, NOPE:] = turned(d_query[:, NOPE:], cos_ref[...], -sin_ref[...]).astype(jnp.bfloat16)

    @pl.when(q_step == pl.num_programs(1) - 1)
    def _():
        dkv_ref[:, :NOPE] = dk_acc[:, :NOPE].astype(jnp.bfloat16)
        dkv_ref[:, NOPE:] = dv_acc[...].astype(jnp.bfloat16)

    @pl.when((q_step == pl.num_programs(1) - 1) & (head == pl.num_programs(0) - 1))
    def _():
        dkr_ref[...] = dk_acc[:, NOPE:].astype(jnp.bfloat16)


def attn_backward(my_ctx, query, keyval, kv_all, d_mixed, mixed, lse_rows, cosines, sines, scale):
    block_rows = query.shape[0]
    seq_len = keyval.shape[0]
    heads = query.shape[1] // 256
    grid_spec = pltpu.PrefetchScalarGridSpec(
        num_scalar_prefetch=1,
        grid=(heads, block_rows // KCHUNK),
        in_specs=[
            pl.BlockSpec((KCHUNK, 256), lambda h, i, c: (i, h)),
            pl.BlockSpec((seq_len, NOPE), lambda h, i, c: (0, 2 * h)),
            pl.BlockSpec((seq_len, 128), lambda h, i, c: (0, RANK // 128)),
            pl.BlockSpec((seq_len, VDIM), lambda h, i, c: (0, 2 * h + 1)),
            pl.BlockSpec((KCHUNK, VDIM), lambda h, i, c: (i, h)),
            pl.BlockSpec((KCHUNK, VDIM), lambda h, i, c: (i, h)),
            pl.BlockSpec((1, 1, KCHUNK), lambda h, i, c: (h, 0, i)),
            pl.BlockSpec((KCHUNK, 128), lambda h, i, c: (i, 0)),
            pl.BlockSpec((KCHUNK, 128), lambda h, i, c: (i, 0)),
        ],
        out_specs=[
            pl.BlockSpec((KCHUNK, 256), lambda h, i, c: (i, h)),
            pl.BlockSpec((seq_len, 256), lambda h, i, c: (0, h)),
            pl.BlockSpec((seq_len, 128), lambda h, i, c: (0, 0)),
        ],
        scratch_shapes=[
            pltpu.VMEM((seq_len, 256), jnp.float32),
            pltpu.VMEM((seq_len, VDIM), jnp.float32),
        ],
    )
    return pl.pallas_call(
        functools.partial(attn_bwd_kernel, scale=scale, block_rows=block_rows),
        grid_spec=grid_spec,
        out_shape=[
            jax.ShapeDtypeStruct((block_rows, heads * 256), jnp.bfloat16),
            jax.ShapeDtypeStruct((seq_len, heads * 256), jnp.bfloat16),
            jax.ShapeDtypeStruct((seq_len, 128), jnp.bfloat16),
        ],
        compiler_params=params(),
        cost_estimate=cost(9, 10),
        name="attn_backward",
    )(
        jnp.full((1,), my_ctx, jnp.int32),
        query, keyval, kv_all, keyval, d_mixed, mixed, lse_rows, cosines, sines,
    )


def resid_kernel(at_ref, x_ref, gain_ref, *refs, n_parts, n_slots):
    parts = refs[:n_parts]
    slots = refs[n_parts : n_parts + n_slots]
    hidden_ref, own_ref, acc_ref = refs[n_parts + n_slots :]
    blk = x_ref.shape[0]
    acc = x_ref[...].astype(jnp.float32)
    for k, slot in enumerate(slots):
        source = at_ref[k]
        weight = jnp.concatenate([part[source] for part in parts], 0)
        acc = acc + matmul(slot[...], weight)
    acc_ref[...] = acc
    hidden_ref[...] = (acc * rms_scale(acc) * gain_ref[...]).astype(jnp.bfloat16)
    own_start = at_ref[n_slots]

    @pl.when(pl.program_id(0) == own_start // blk)
    def _():
        own_ref[...] = acc_ref[pl.ds(pl.multiple_of(own_start % blk, ROWS), ROWS), :]


def resid_and_hidden(at, x, gain, parts, slots):
    rows = x.shape[0]
    blk = 512
    grid_spec = pltpu.PrefetchScalarGridSpec(
        num_scalar_prefetch=1,
        grid=(rows // blk,),
        in_specs=[pl.BlockSpec((blk, D), lambda i, a: (i, 0)), whole((1, D))]
        + [whole(part.shape) for part in parts]
        + [pl.BlockSpec((blk, slot.shape[1]), lambda i, a: (i, 0)) for slot in slots],
        out_specs=[pl.BlockSpec((blk, D), lambda i, a: (i, 0)), whole((ROWS, D))],
        scratch_shapes=[pltpu.VMEM((blk, D), jnp.float32)],
    )
    return pl.pallas_call(
        functools.partial(resid_kernel, n_parts=len(parts), n_slots=len(slots)),
        grid_spec=grid_spec,
        out_shape=[
            jax.ShapeDtypeStruct((rows, D), jnp.bfloat16),
            jax.ShapeDtypeStruct((ROWS, D), jnp.float32),
        ],
        compiler_params=params(),
        cost_estimate=cost(8.6, 24),
        name="resid_and_hidden",
    )(at, x, gain.reshape(1, D), *parts, *slots)


def forward_kernel(x_ref, gate_w_ref, up_w_ref, act_ref, for_gate_ref, for_up_ref, gate_acc):
    phase = pl.program_id(1)

    @pl.when(phase == 0)
    def _():
        gate_acc[...] = matmul(x_ref[0], gate_w_ref[0])

    @pl.when(phase == 1)
    def _():
        up = matmul(x_ref[0], up_w_ref[0])
        silu, slope = silu_parts(gate_acc[...])
        act_ref[0] = (silu * up).astype(jnp.bfloat16)
        for_gate_ref[0] = (up * slope).astype(jnp.bfloat16)
        for_up_ref[0] = silu.astype(jnp.bfloat16)


def per_expert(shape):
    rest = (0,) * (len(shape) - 1)
    return pl.BlockSpec((1,) + shape[1:], lambda e, i: (e,) + rest)


def experts_forward(expert_in, gate, up):
    ff = gate.shape[2]
    hidden = jax.ShapeDtypeStruct((EXP_DEV, CAPB, ff), jnp.bfloat16)
    return pl.pallas_call(
        forward_kernel,
        grid=(EXP_DEV, 2),
        in_specs=[per_expert(expert_in.shape), per_expert(gate.shape), per_expert(up.shape)],
        out_specs=[per_expert(hidden.shape)] * 3,
        out_shape=[hidden] * 3,
        scratch_shapes=[pltpu.VMEM((CAPB, ff), jnp.float32)],
        compiler_params=params(),
        cost_estimate=cost(12, 36),
        name="experts_forward",
    )(expert_in, gate, up)


def backward_kernel(
    dout_ref, for_gate_ref, for_up_ref, down_ref, gate_ref, up_ref, d_gate_ref, d_up_ref, din_ref
):
    phase = pl.program_id(1)

    @pl.when(phase == 0)
    def _():
        d_act = times_transposed(dout_ref[0], down_ref[0])
        d_gate_ref[0] = (d_act * for_gate_ref[0].astype(jnp.float32)).astype(jnp.bfloat16)
        d_up_ref[0] = (d_act * for_up_ref[0].astype(jnp.float32)).astype(jnp.bfloat16)

    @pl.when(phase > 0)
    def _():
        total = times_transposed(d_gate_ref[0], gate_ref[0])
        total = total + times_transposed(d_up_ref[0], up_ref[0])
        din_ref[0] = total.astype(jnp.bfloat16)


def experts_backward(d_out, for_gate, for_up, gate, up, down):
    ff = gate.shape[2]
    cols = D // 2
    hidden = jax.ShapeDtypeStruct((EXP_DEV, CAPB, ff), jnp.bfloat16)
    half_rows = pl.BlockSpec((1, cols, ff), lambda e, i: (e, jnp.maximum(i - 1, 0), 0))
    return pl.pallas_call(
        backward_kernel,
        grid=(EXP_DEV, 3),
        in_specs=[
            per_expert(d_out.shape), per_expert(hidden.shape), per_expert(hidden.shape),
            per_expert(down.shape), half_rows, half_rows,
        ],
        out_specs=[
            per_expert(hidden.shape), per_expert(hidden.shape),
            pl.BlockSpec((1, CAPB, cols), lambda e, i: (e, 0, jnp.maximum(i - 1, 0))),
        ],
        out_shape=[hidden, hidden, jax.ShapeDtypeStruct((EXP_DEV, CAPB, D), jnp.bfloat16)],
        compiler_params=params(),
        cost_estimate=cost(18, 50),
        name="experts_backward",
    )(d_out, for_gate, for_up, down, gate, up)


def out_kernel(act_ref, mass_ref, down_ref, out_ref):
    out_ref[0] = (matmul(act_ref[0], down_ref[0]) * mass_ref[0]).astype(jnp.bfloat16)


def experts_out(act, mass, down):
    ff = act.shape[2]
    cols = D // 2
    return pl.pallas_call(
        out_kernel,
        grid=(EXP_DEV, 2),
        in_specs=[
            per_expert(act.shape), per_expert(mass.shape),
            pl.BlockSpec((1, ff, cols), lambda e, i: (e, 0, i)),
        ],
        out_specs=pl.BlockSpec((1, CAPB, cols), lambda e, i: (e, 0, i)),
        out_shape=jax.ShapeDtypeStruct((EXP_DEV, CAPB, D), jnp.bfloat16),
        compiler_params=params(),
        cost_estimate=cost(6, 20),
        name="experts_out",
    )(act, mass, down)


def products_kernel(*refs):
    out_ref = refs[-1]
    total = None
    for k in range(len(refs) // 2):
        product = matmul(refs[2 * k][...], refs[2 * k + 1][...])
        total = product if total is None else total + product
    out_ref[...] = total.astype(out_ref.dtype)


def sum_of_products(name, terms, gflop, mbytes):
    rows, blk = terms[0][0].shape[0], 512
    specs, flat = [], []
    for left, right in terms:
        specs += [whole(left.shape), pl.BlockSpec((right.shape[0], blk), lambda i: (0, i))]
        flat += [left, right]
    return pl.pallas_call(
        products_kernel,
        grid=(D // blk,),
        in_specs=specs,
        out_specs=pl.BlockSpec((rows, blk), lambda i: (0, i)),
        out_shape=jax.ShapeDtypeStruct((rows, D), jnp.bfloat16),
        compiler_params=params(),
        cost_estimate=cost(gflop, mbytes),
        name=name,
    )(*flat)


def latent_kernel(at_ref, dkv_ref, kvw_ref, dkr_ref, *refs):
    outs, tile = refs[:-1], refs[-1]
    tile[:, :RANK] = times_transposed(dkv_ref[...], kvw_ref[...]).astype(jnp.bfloat16)
    tile[:, RANK:] = dkr_ref[...]
    for k, out in enumerate(outs):
        out[0] = tile[pl.ds(pl.multiple_of(at_ref[k], ROWS), ROWS), :]


def latent_parts(at, d_kv, keyval_weight, d_krope, n_ctx):
    blk = d_kv.shape[0] // n_ctx
    row_spec = lambda width: pl.BlockSpec((blk, width), lambda i, a: (i, 0))
    grid_spec = pltpu.PrefetchScalarGridSpec(
        num_scalar_prefetch=1,
        grid=(n_ctx,),
        in_specs=[
            row_spec(d_kv.shape[1]),
            pl.BlockSpec(keyval_weight.shape, lambda i, a: (0, 0)),
            row_spec(128),
        ],
        out_specs=[pl.BlockSpec((1, ROWS, RANK + 128), lambda i, a: (i, 0, 0))] * (blk // ROWS),
        scratch_shapes=[pltpu.VMEM((blk, RANK + 128), jnp.bfloat16)],
    )
    return pl.pallas_call(
        latent_kernel,
        grid_spec=grid_spec,
        out_shape=[jax.ShapeDtypeStruct((n_ctx, ROWS, RANK + 128), jnp.bfloat16)] * (blk // ROWS),
        compiler_params=params(),
        cost_estimate=cost(1, 6),
        name="latent_parts",
    )(at, d_kv, keyval_weight, d_krope)


def turn(values, axis, step):
    size = lax.axis_size(axis)
    return lax.ppermute(values, axis, [(i, (i + step) % size) for i in range(size)])


def move(values, flip):
    pairs = [(i, i ^ flip) for i in range(lax.axis_size("experts"))]
    return lax.ppermute(values, "experts", pairs)


def gather_slots(values):
    far = move(values, 4)
    near = move(values, 2)
    both = move(far, 2)
    slots = {}
    for k, here in ((0, values), (2, near), (4, far), (6, both)):
        slots[k], slots[k + 1] = here, move(here, 1)
    return [slots[k] for k in range(8)]


def scatter_sum(parts):
    def pair(k):
        return parts[k].astype(jnp.float32) + move(parts[k + 1], 1).astype(jnp.float32)

    def sent(values, flip):
        return move(values.astype(jnp.bfloat16), flip).astype(jnp.float32)

    both = sent(pair(6), 2)
    far = sent(pair(4) + both, 4)
    near = sent(pair(2), 2)
    return pair(0) + near + far


def butterfly(values, axis):
    size = lax.axis_size(axis)
    span = 1
    while span < size:
        pairs = [(i, i ^ span) for i in range(size)]
        values = values + lax.ppermute(values, axis, pairs)
        span *= 2
    return values


def gather_quarters(shard, dim):
    return lax.all_gather(shard, ("context", "dp"), axis=dim, tiled=True)


def after(values, *others):
    return lax.optimization_barrier((values,) + others)[0]


def grad_stages(product, split, dim):
    n_ctx, n_dp = lax.axis_size("context"), lax.axis_size("dp")
    my_ctx, my_dp = lax.axis_index("context"), lax.axis_index("dp")
    width = split.shape[2] // (n_ctx * n_dp)
    part = lambda c, d: lax.dynamic_slice_in_dim(split, (c * n_dp + d) * width, width, 2)
    got = []
    for j in range(1, n_dp):
        there = (my_dp + j) % n_dp
        sent = product(jnp.concatenate([part(c, there) for c in range(n_ctx)], 2))
        got.append(turn(sent.astype(jnp.bfloat16), "dp", j))

    def near(c):
        total = product(part(c, my_dp))
        for other in got:
            total = total + lax.dynamic_slice_in_dim(other, c * width, width, dim).astype(
                jnp.float32
            )
        return total

    sums = [near((my_ctx + k) % n_ctx).astype(jnp.bfloat16) for k in range(1, n_ctx)]
    heard = [turn(there, "context", k + 1) for k, there in enumerate(sums)]
    return sums, heard, near(my_ctx)


def finish_grad(heard, own):
    for other in heard:
        own = own + other.astype(jnp.float32)
    return own


def sum_weight_grad(grad, dim=0):
    n_ctx, n_dp = lax.axis_size("context"), lax.axis_size("dp")
    my_dp = lax.axis_index("dp")
    width = grad.shape[dim] // n_dp
    part = lambda j: lax.dynamic_slice_in_dim(grad, (my_dp + j) % n_dp * width, width, dim)
    own = part(0)
    for j in range(1, n_dp):
        own = own + turn(part(j).astype(jnp.bfloat16), "dp", j).astype(jnp.float32)
    own = own.astype(jnp.bfloat16)
    if n_ctx == 2:
        own = own.astype(jnp.float32) + turn(own, "context", 1).astype(jnp.float32)
        own = own.astype(jnp.bfloat16)
    else:
        own = lax.psum(own, "context")
    total = jnp.zeros(grad.shape, jnp.bfloat16)
    for j in range(n_dp):
        piece = turn(own, "dp", j) if j else own
        at = (my_dp + n_dp - j) % n_dp
        total = lax.dynamic_update_slice_in_dim(total, piece, at * width, dim)
    return total.astype(jnp.float32)


def local(
    layer_input,
    routes,
    route_weights,
    query_weight,
    latent_weight,
    keyval_weight,
    output_weight,
    attn_gain,
    latent_gain,
    ffn_gain,
    shared_gate,
    shared_up,
    shared_down,
    expert_gate,
    expert_up,
    expert_down,
    cotangent,
):
    n_exp = lax.axis_size("experts")
    n_ctx = lax.axis_size("context")
    n_dp = lax.axis_size("dp")
    my_exp = lax.axis_index("experts")
    my_ctx = lax.axis_index("context")
    my_dp = lax.axis_index("dp")
    block_rows = layer_input.shape[2]
    heads_dev = query_weight.shape[1] // (NOPE + ROPE)
    scale = (NOPE + ROPE) ** (-0.5)
    low = jnp.bfloat16
    route_ids = routes.reshape(block_rows, TOPK)
    route_mass = route_weights.reshape(block_rows, TOPK)
    grad_out = cotangent.reshape(block_rows, D)
    own_start = my_exp * ROWS

    def own_rows(values):
        return lax.dynamic_slice_in_dim(values, own_start, ROWS, 0)

    full_gate = gather_quarters(expert_gate, 1)
    full_up = gather_quarters(expert_up, 1)
    full_down = gather_quarters(expert_down, 2)
    lane = jnp.arange(128, dtype=jnp.int32)[None, :]
    freqs = ROPE_BASE ** (-(lane % (ROPE // 2)).astype(jnp.float32) * 2.0 / ROPE)

    def tables(positions):
        turns = positions.astype(jnp.float32)[:, None] * freqs
        sines = jnp.sin(turns)
        sines = jnp.where(lane < ROPE // 2, -sines, sines)
        return (jnp.where(lane < ROPE, jnp.cos(turns), 0.0), jnp.where(lane < ROPE, sines, 0.0))

    query_pos = my_ctx * block_rows + jnp.arange(block_rows, dtype=jnp.int32)
    cos_q, sin_q = tables(query_pos)
    x_block = layer_input.reshape(block_rows, D)
    latent_turned = latent_weight.T
    normed, query, kv_low = front(
        x_block, attn_gain, query_weight, latent_turned, latent_gain, cos_q, sin_q
    )
    ow_rows = output_weight.shape[0] // n_dp
    ow_mine = lax.dynamic_slice_in_dim(output_weight, my_dp * ow_rows, ow_rows, 0)
    ow_mine = after(ow_mine, query)
    ow_near = jnp.zeros((n_exp, ow_rows, D), low)
    for k, rows in enumerate(gather_slots(ow_mine)):
        ow_near = lax.dynamic_update_slice_in_dim(ow_near, rows[None], my_exp ^ k, 0)
    ow_parts = [turn(ow_near, "dp", j) if j else ow_near for j in range(n_dp)]

    kv_blocks = [kv_low]
    for k in range(1, n_ctx):
        pairs = [(i, i + k) for i in range(n_ctx - k)]
        kv_blocks.append(lax.ppermute(kv_low, "context", pairs))
    kv_all = jnp.concatenate(kv_blocks, 0)
    latent_all = kv_all[:, :RANK]
    expanded = matmul(latent_all, keyval_weight).astype(low)
    mixed, logsums = attn_forward(my_ctx, query, expanded, kv_all, scale)

    def head_turn(values, back):
        step = my_dp * VDIM * (heads_dev // n_dp)
        width = values.shape[1]
        twice = jnp.concatenate([values, values], 1)
        start = (width - step) % width if back else step
        return lax.dynamic_slice_in_dim(twice, start, width, 1)

    mixed_slots = gather_slots(head_turn(mixed, False))
    slot_at = jnp.stack([my_exp ^ k for k in range(n_exp)] + [own_start]).astype(jnp.int32)
    hidden_in, resid_own = resid_and_hidden(slot_at, x_block, ffn_gain, ow_parts, mixed_slots)
    scale_mid_own = rms_scale(resid_own)

    expert_ids = my_exp * EXP_DEV + jnp.arange(EXP_DEV, dtype=jnp.int32)
    chosen = route_ids[:, :, None] == expert_ids[None, None, :]
    member = jnp.any(chosen, 1)
    mass = jnp.sum(jnp.where(chosen, route_mass[:, :, None], 0.0), 1)
    earlier = (
        jnp.arange(block_rows, dtype=jnp.int32)[:, None]
        > jnp.arange(block_rows, dtype=jnp.int32)[None, :]
    ).astype(low)
    rank = matmul(earlier, member.astype(low)).astype(jnp.int32)
    slot_of = jnp.where(member, rank, -1).T
    taken = slot_of[:, None, :] == jnp.arange(CAPB, dtype=jnp.int32)[None, :, None]
    slot_mass = jnp.sum(jnp.where(taken, mass.T[:, None, :], 0.0), -1)
    pick = taken.astype(low).reshape(EXP_DEV * CAPB, block_rows)
    spread = (
        jnp.where(member, rank, -1)[:, :, None] == jnp.arange(CAPB, dtype=jnp.int32)[None, None, :]
    ).astype(low).reshape(block_rows, EXP_DEV * CAPB)

    d_out = (
        (matmul(pick, grad_out) * slot_mass.reshape(-1, 1)).astype(low).reshape(EXP_DEV, CAPB, D)
    )
    expert_in = matmul(pick, hidden_in).astype(low).reshape(EXP_DEV, CAPB, D)
    act_e, for_gate, for_up = experts_forward(expert_in, full_gate, full_up)
    down_sums, down_heard, down_own = grad_stages(
        lambda part: jnp.einsum("ecf,ecd->efd", act_e, part, preferred_element_type=jnp.float32),
        d_out,
        2,
    )
    d_out, *down_sums = lax.optimization_barrier((d_out, *down_sums))
    d_gate_e, d_up_e, d_in_e = experts_backward(
        d_out, for_gate, for_up, full_gate, full_up, full_down
    )
    out_e = experts_out(act_e, slot_mass[:, :, None], full_down)
    gate_sums, gate_heard, gate_own = grad_stages(
        lambda part: jnp.einsum("ecd,ecf->edf", part, d_gate_e, preferred_element_type=jnp.float32),
        expert_in,
        1,
    )
    up_sums, up_heard, up_own = grad_stages(
        lambda part: jnp.einsum("ecd,ecf->edf", part, d_up_e, preferred_element_type=jnp.float32),
        expert_in,
        1,
    )

    gate_s = matmul(hidden_in, shared_gate)
    up_s = matmul(hidden_in, shared_up)
    silu_s, slope_s = silu_parts(gate_s)
    act_s = (silu_s * up_s).astype(low)
    d_act_s = times_transposed(grad_out, shared_down)
    d_up_s = (d_act_s * silu_s).astype(low)
    d_gate_s = (d_act_s * up_s * slope_s).astype(low)
    slots_all = EXP_DEV * CAPB
    d_hidden_part = sum_of_products(
        "d_hidden_part",
        [
            (d_gate_s, shared_gate.T),
            (d_up_s, shared_up.T),
            (spread, d_in_e.reshape(slots_all, D)),
        ],
        7.3, 16,
    )
    d_hidden_own = lax.psum_scatter(d_hidden_part, "experts", scatter_dimension=0, tiled=True)
    ffn_part = sum_of_products(
        "ffn_part",
        [(act_s, shared_down), (spread, out_e.reshape(slots_all, D))],
        5.8, 14,
    )
    d_hidden_own, ffn_part, down_heard, gate_heard, up_sums, down_own, gate_own, up_own = (
        lax.optimization_barrier(
            (d_hidden_own, ffn_part, down_heard, gate_heard, up_sums, down_own, gate_own, up_own)
        )
    )
    d_hidden_own = d_hidden_own.astype(jnp.float32)
    grad_own = own_rows(grad_out).astype(jnp.float32)

    def norm_mid(values_in):
        return values_in * rms_scale(values_in) * ffn_gain

    _, mid_pull = jax.vjp(norm_mid, resid_own)
    d_resid_own = grad_own + mid_pull(d_hidden_own)[0]
    d_ffn_gain = jnp.sum(d_hidden_own * resid_own * scale_mid_own, 0)
    d_resid_low = d_resid_own.astype(low)
    d_mixed_parts = [
        times_transposed(d_resid_low, part.reshape(-1, D))
        .astype(low)
        .reshape(ROWS, n_exp, -1)
        .transpose(1, 0, 2)
        for part in ow_parts
    ]
    d_mixed = lax.all_to_all(jnp.concatenate(d_mixed_parts, 2), "experts", 0, 0, tiled=True)
    d_mixed = after(d_mixed, up_heard)
    d_mixed = head_turn(d_mixed.reshape(block_rows, heads_dev * VDIM), True)

    d_query, d_kv, d_krope = attn_backward(
        my_ctx, query, expanded, kv_all, d_mixed, mixed, logsums, cos_q, sin_q, scale
    )
    target_rows = jnp.stack([(my_exp ^ k) * ROWS for k in range(n_exp)]).astype(jnp.int32)
    d_lat_blocks = scatter_sum(latent_parts(target_rows, d_kv, keyval_weight, d_krope, n_ctx))
    d_comp_own = d_lat_blocks[0]
    for k in range(1, n_ctx):
        pairs = [(i, i - k) for i in range(k, n_ctx)]
        d_comp_own = d_comp_own + lax.ppermute(
            d_lat_blocks[k].astype(low), "context", pairs
        ).astype(jnp.float32)
    head_width = NOPE + ROPE
    d_query_low = jnp.concatenate(
        [d_query[:, 256 * h : 256 * h + head_width] for h in range(heads_dev)], 1
    )
    d_norm_part = times_transposed(d_query_low, query_weight).astype(low)
    d_norm_own = lax.psum_scatter(
        d_norm_part, "experts", scatter_dimension=0, tiled=True
    ).astype(jnp.float32)

    own_pos = my_ctx * block_rows + own_start + jnp.arange(ROWS, dtype=jnp.int32)
    cos_k, sin_k = angles(own_pos)
    own_normed = own_rows(normed)

    def latent_fn(comp_rows, lat_gain):
        lat_part = comp_rows[:, :RANK] * rms_scale(comp_rows[:, :RANK]) * lat_gain
        return jnp.concatenate([lat_part, rotate(comp_rows[:, RANK:], cos_k, sin_k)], -1)

    _, kv_pull = jax.vjp(latent_fn, matmul(own_normed, latent_weight), latent_gain)
    d_comp, d_lat_gain = kv_pull(d_comp_own[:, : RANK + ROPE])
    d_comp_low = d_comp.astype(low)
    d_norm_total = d_norm_own + times_transposed(d_comp_low, latent_weight)

    def norm_in(values_in, gain_in):
        return values_in * rms_scale(values_in) * gain_in

    _, in_pull = jax.vjp(norm_in, own_rows(x_block).astype(jnp.float32), attn_gain)
    d_in_rows, d_attn_gain = in_pull(d_norm_total)
    input_grad = (d_resid_own + d_in_rows).reshape(1, 1, ROWS, D)

    ffn_out = lax.psum_scatter(
        ffn_part, "experts", scatter_dimension=0, tiled=True
    ).astype(jnp.float32)
    layer_output = (resid_own + ffn_out).astype(low).reshape(1, 1, ROWS, D)

    expert_gate_grad = finish_grad(gate_heard, gate_own)
    expert_up_grad = finish_grad(up_heard, up_own)
    expert_down_grad = finish_grad(down_heard, down_own)

    shared_width = act_s.shape[1]
    d_shared = jnp.concatenate([d_gate_s, d_up_s], 1)
    shared_grads = sum_weight_grad(
        jnp.concatenate(
            [contract_rows(d_shared, hidden_in), contract_rows(act_s, grad_out)], 0
        ),
        1,
    )
    shared_gate_grad = shared_grads[:shared_width].T
    shared_up_grad = shared_grads[shared_width : 2 * shared_width].T
    shared_down_grad = shared_grads[2 * shared_width :]
    query_grad = sum_weight_grad(contract_rows(normed, d_query_low))
    keyval_grad = sum_weight_grad(contract_rows(latent_all, d_kv))
    d_resid_block = lax.all_gather(d_resid_low, "experts", axis=0, tiled=True)
    output_grad = sum_weight_grad(contract_rows(mixed, d_resid_block))

    grad_latent = contract_rows(d_comp_low, own_normed)
    lat_half_cols = D // n_dp
    lat_cols = lat_half_cols // n_exp

    def columns(values, at, width):
        return lax.dynamic_slice_in_dim(values, at, width, 1)

    lat_half = columns(grad_latent, my_dp * lat_half_cols, lat_half_cols)
    for j in range(1, n_dp):
        sent = columns(grad_latent, (my_dp + j) % n_dp * lat_half_cols, lat_half_cols)
        lat_half = lat_half + turn(sent.astype(low), "dp", j).astype(jnp.float32)
    lat_half = lat_half.astype(low)
    lat_own = scatter_sum([columns(lat_half, (my_exp ^ k) * lat_cols, lat_cols) for k in range(n_exp)])
    lat_own = butterfly(lat_own, "context").astype(low)
    lat_half = jnp.zeros((RANK + ROPE, lat_half_cols), low)
    for k, part in enumerate(gather_slots(lat_own)):
        lat_half = lax.dynamic_update_slice_in_dim(lat_half, part, (my_exp ^ k) * lat_cols, 1)
    latent_grad = jnp.zeros((RANK + ROPE, D), low)
    for j in range(n_dp):
        piece = turn(lat_half, "dp", j) if j else lat_half
        at = (my_dp + n_dp - j) % n_dp
        latent_grad = lax.dynamic_update_slice_in_dim(latent_grad, piece, at * lat_half_cols, 1)
    latent_grad = latent_grad.astype(jnp.float32).T

    gains = jnp.concatenate([d_attn_gain, d_lat_gain, d_ffn_gain])
    for axis in ("dp", "context", "experts"):
        gains = butterfly(gains, axis)
    attn_gain_grad = gains[:D]
    latent_gain_grad = gains[D : D + RANK]
    ffn_gain_grad = gains[D + RANK :]
    return (
        layer_output,
        input_grad,
        query_grad,
        latent_grad,
        keyval_grad,
        output_grad,
        attn_gain_grad,
        latent_gain_grad,
        ffn_gain_grad,
        shared_gate_grad,
        shared_up_grad,
        shared_down_grad,
        expert_gate_grad,
        expert_up_grad,
        expert_down_grad,
    )


def solution(mesh):
    in_specs = (
        P("dp", "context", None, None),
        P("dp", "context", None, None),
        P("dp", "context", None, None),
        P(None, "experts"),
        P(),
        P(None, "experts"),
        P("experts", None),
        P(),
        P(),
        P(),
        P(None, "experts"),
        P(None, "experts"),
        P("experts", None),
        P("experts", ("context", "dp"), None),
        P("experts", ("context", "dp"), None),
        P("experts", None, ("context", "dp")),
        P("dp", "context", None, None),
    )
    out_specs = (
        P("dp", "context", "experts", None),
        P("dp", "context", "experts", None),
        P(None, "experts"),
        P(),
        P(None, "experts"),
        P("experts", None),
        P(),
        P(),
        P(),
        P(None, "experts"),
        P(None, "experts"),
        P("experts", None),
        P("experts", ("context", "dp"), None),
        P("experts", ("context", "dp"), None),
        P("experts", None, ("context", "dp")),
    )
    return jax.shard_map(local, mesh=mesh, in_specs=in_specs, out_specs=out_specs, check_vma=False)
```

```python
import functools

import jax
import jax.numpy as jnp
from jax import lax
from jax.experimental import pallas as pl
from jax.experimental.pallas import tpu as pltpu
from jax.sharding import PartitionSpec as P

D = 2048
NOPE = 128
ROPE = 64
VDIM = 128
RANK = 512
TOPK = 6
EXP_DEV = 2
ROWS = 128
CAPB = 512


EPSILON = 1e-06
ROPE_BASE = 50000.0
MASKED = -1e30


def angles(positions):
    half_width = ROPE // 2
    freqs_table = ROPE_BASE ** (-jnp.arange(half_width, dtype=jnp.float32) * 2.0 / ROPE)
    turned = positions.astype(jnp.float32)[:, None] * freqs_table[None, :]
    return (jnp.cos(turned), jnp.sin(turned))


def rotate(values_in, cosines, sines):
    half_width = values_in.shape[-1] // 2
    first_half = values_in[..., :half_width]
    second_half = values_in[..., half_width:]
    return jnp.concatenate(
        [first_half * cosines - second_half * sines, second_half * cosines + first_half * sines], -1
    )


def rms_scale(values_in):
    return lax.rsqrt(jnp.mean(values_in * values_in, -1, keepdims=True) + EPSILON)


def matmul(left_side, right_side):
    return jnp.dot(left_side, right_side, preferred_element_type=jnp.float32)


def contract_rows(left_side, right_side):
    return lax.dot_general(
        left_side, right_side, (((0,), (0,)), ((), ())), preferred_element_type=jnp.float32
    )


def times_transposed(left_side, right_side):
    return lax.dot_general(
        left_side, right_side, (((1,), (1,)), ((), ())), preferred_element_type=jnp.float32
    )


def silu_parts(gate_vals):
    sigmoid_g = jax.nn.sigmoid(gate_vals)
    return (gate_vals * sigmoid_g, sigmoid_g * (1.0 + gate_vals * (1.0 - sigmoid_g)))


OFFLOAD = {"d_hidden": True, "ffn_part": False, "d_norm": True, "d_resid": True}
PLACES = {"down0": "spread", "down1": "act", "both0": "mix", "both1": "lat_own", "down_own": "ffn", "both_own": "ffn", "shared_own": "ffn", "shared_heard": "comp", "d_norm": "lat_own"}
KCHUNK = 512
VMEM_LIMIT = 56 * 2**20


def params():
    return pltpu.CompilerParams(vmem_limit_bytes=VMEM_LIMIT)


def cost(gflop, mbytes):
    return pl.CostEstimate(
        flops=int(gflop * 1e9), bytes_accessed=int(mbytes * 1e6), transcendentals=0
    )


def whole(shape):
    zeros = (0,) * len(shape)
    return pl.BlockSpec(shape, lambda *at: zeros)


def turned(tile, cosines, sines):
    lane = lax.broadcasted_iota(jnp.int32, tile.shape, 1)
    half_width = ROPE // 2
    other = jnp.where(
        lane < half_width, pltpu.roll(tile, 128 - half_width, 1), pltpu.roll(tile, half_width, 1)
    )
    return tile * cosines + other * sines


def front_kernel(x_ref, gain_ref, wq_ref, wl_ref, lgain_ref, cos_ref, sin_ref, normed_ref, q_ref, kv_ref):
    x = x_ref[...].astype(jnp.float32)
    normed = (x * rms_scale(x) * gain_ref[...]).astype(jnp.bfloat16)
    normed_ref[...] = normed
    cosines, sines = cos_ref[...], sin_ref[...]
    low_part = times_transposed(normed, wl_ref[:RANK, :])
    kv_ref[:, :RANK] = (low_part * rms_scale(low_part) * lgain_ref[...]).astype(jnp.bfloat16)
    rope_rows = jnp.concatenate([wl_ref[RANK:, :], jnp.zeros((128 - ROPE, D), jnp.bfloat16)], 0)
    rope_part = times_transposed(normed, rope_rows)
    kv_ref[:, RANK:] = turned(rope_part, cosines, sines).astype(jnp.bfloat16)
    raw = matmul(normed, wq_ref[...])
    width = raw.shape[1]
    for head in range(width // (NOPE + ROPE)):
        start = head * (NOPE + ROPE)
        here = pltpu.roll(raw, width - start, 1) if start else raw
        q_ref[:, head * 256 : head * 256 + NOPE] = here[:, :NOPE].astype(jnp.bfloat16)
        q_ref[:, head * 256 + NOPE : head * 256 + 256] = turned(
            here[:, NOPE : NOPE + 128], cosines, sines
        ).astype(jnp.bfloat16)


def front(x, gain, query_weight, latent_turned, lat_gain, cosines, sines):
    rows = x.shape[0]
    blk = 512
    heads = query_weight.shape[1] // (NOPE + ROPE)
    row_spec = lambda width: pl.BlockSpec((blk, width), lambda i: (i, 0))
    return pl.pallas_call(
        front_kernel,
        grid=(rows // blk,),
        in_specs=[
            row_spec(D), whole((1, D)), whole(query_weight.shape), whole(latent_turned.shape),
            whole((1, RANK)), row_spec(128), row_spec(128),
        ],
        out_specs=[row_spec(D), row_spec(heads * 256), row_spec(RANK + 128)],
        out_shape=[
            jax.ShapeDtypeStruct((rows, D), jnp.bfloat16),
            jax.ShapeDtypeStruct((rows, heads * 256), jnp.bfloat16),
            jax.ShapeDtypeStruct((rows, RANK + 128), jnp.bfloat16),
        ],
        compiler_params=params(),
        cost_estimate=cost(4.5, 16),
        name="front",
    )(x, gain.reshape(1, D), query_weight, latent_turned, lat_gain.reshape(1, RANK), cosines, sines)


def to_row(column_tile):
    ones = jnp.ones((8, 128), jnp.float32)
    return lax.dot_general(
        ones, column_tile, (((1,), (1,)), ((), ())),
        precision=lax.Precision.HIGHEST, preferred_element_type=jnp.float32,
    )[0:1]


def attn_fwd_kernel(ctx_ref, q_ref, kn_ref, kr_ref, v_ref, out_ref, lse_ref, *, scale, block_rows):
    q_step = pl.program_id(1)
    rows = q_ref.shape[0]
    query = q_ref[...]

    def step(chunk, carry, masked):
        row_max, denom, acc = carry
        at = pl.ds(pl.multiple_of(chunk * KCHUNK, KCHUNK), KCHUNK)
        keys = jnp.concatenate([kn_ref[at, :], kr_ref[at, :]], -1)
        scores = times_transposed(query, keys) * scale
        if masked:
            row_at = lax.broadcasted_iota(jnp.int32, scores.shape, 0)
            col_at = lax.broadcasted_iota(jnp.int32, scores.shape, 1)
            scores = jnp.where(col_at <= row_at, scores, MASKED)
        new_max = jnp.maximum(row_max, jnp.max(scores, -1, keepdims=True))
        shrink = jnp.exp(row_max - new_max)
        terms = jnp.exp(scores - new_max)
        denom = denom * shrink + jnp.sum(terms, -1, keepdims=True)
        acc = acc * shrink + matmul(terms.astype(jnp.bfloat16), v_ref[at, :])
        return new_max, denom, acc

    carry = (
        jnp.full((rows, 1), MASKED, jnp.float32),
        jnp.zeros((rows, 1), jnp.float32),
        jnp.zeros((rows, VDIM), jnp.float32),
    )
    carry = step(q_step, carry, True)
    carry = lax.fori_loop(0, q_step, lambda i, c: step(i, c, False), carry)
    per_block = block_rows // KCHUNK
    carry = lax.fori_loop(
        per_block, per_block * (1 + ctx_ref[0]), lambda i, c: step(i, c, False), carry
    )
    row_max, denom, acc = carry
    out_ref[...] = (acc / denom).astype(jnp.bfloat16)
    lane = lax.broadcasted_iota(jnp.int32, (rows, 128), 1)
    lse_ref[0] = to_row(jnp.where(lane == 0, row_max + jnp.log(denom), 0.0))


def attn_forward(my_ctx, query, keyval, kv_all, scale):
    block_rows = query.shape[0]
    seq_len = keyval.shape[0]
    heads = query.shape[1] // 256
    grid_spec = pltpu.PrefetchScalarGridSpec(
        num_scalar_prefetch=1,
        grid=(heads, block_rows // KCHUNK),
        in_specs=[
            pl.BlockSpec((KCHUNK, 256), lambda h, i, c: (i, h)),
            pl.BlockSpec((seq_len, NOPE), lambda h, i, c: (0, 2 * h)),
            pl.BlockSpec((seq_len, 128), lambda h, i, c: (0, RANK // 128)),
            pl.BlockSpec((seq_len, VDIM), lambda h, i, c: (0, 2 * h + 1)),
        ],
        out_specs=[
            pl.BlockSpec((KCHUNK, VDIM), lambda h, i, c: (i, h)),
            pl.BlockSpec((1, 1, KCHUNK), lambda h, i, c: (h, 0, i)),
        ],
    )
    return pl.pallas_call(
        functools.partial(attn_fwd_kernel, scale=scale, block_rows=block_rows),
        grid_spec=grid_spec,
        out_shape=[
            jax.ShapeDtypeStruct((block_rows, heads * VDIM), jnp.bfloat16),
            jax.ShapeDtypeStruct((heads, 1, block_rows), jnp.float32),
        ],
        compiler_params=params(),
        cost_estimate=cost(4, 8),
        name="attn_forward",
    )(jnp.full((1,), my_ctx, jnp.int32), query, keyval, kv_all, keyval)


def attn_bwd_kernel(
    ctx_ref, q_ref, kn_ref, kr_ref, v_ref, dmix_ref, mix_ref, lse_ref, cos_ref, sin_ref,
    dq_ref, dkv_ref, dkr_ref, dk_acc, dv_acc, *, scale, block_rows,
):
    head = pl.program_id(0)
    q_step = pl.program_id(1)
    rows = q_ref.shape[0]

    @pl.when(q_step == 0)
    def _():
        dv_acc[...] = jnp.zeros_like(dv_acc)
        dk_acc[:, :NOPE] = jnp.zeros((dk_acc.shape[0], NOPE), jnp.float32)

    @pl.when((q_step == 0) & (head == 0))
    def _():
        dk_acc[:, NOPE:] = jnp.zeros((dk_acc.shape[0], 128), jnp.float32)

    query = q_ref[...]
    dmix = dmix_ref[...]
    lse = lse_ref[0]
    delta = to_row(dmix.astype(jnp.float32) * mix_ref[...].astype(jnp.float32))

    def step(chunk, d_query, masked):
        at = pl.ds(pl.multiple_of(chunk * KCHUNK, KCHUNK), KCHUNK)
        keys = jnp.concatenate([kn_ref[at, :], kr_ref[at, :]], -1)
        scores = times_transposed(keys, query) * scale - lse
        if masked:
            key_at = lax.broadcasted_iota(jnp.int32, scores.shape, 0)
            row_at = lax.broadcasted_iota(jnp.int32, scores.shape, 1)
            scores = jnp.where(key_at <= row_at, scores, MASKED)
        probs = jnp.exp(scores)
        dprob = times_transposed(v_ref[at, :], dmix)
        d_raw = (probs * (dprob - delta) * scale).astype(jnp.bfloat16)
        dv_acc[at, :] += matmul(probs.astype(jnp.bfloat16), dmix)
        dk_acc[at, :] += matmul(d_raw, query)
        return d_query + contract_rows(d_raw, keys)

    d_query = step(q_step, jnp.zeros((rows, 256), jnp.float32), True)
    d_query = lax.fori_loop(0, q_step, lambda i, c: step(i, c, False), d_query)
    per_block = block_rows // KCHUNK
    d_query = lax.fori_loop(
        per_block, per_block * (1 + ctx_ref[0]), lambda i, c: step(i, c, False), d_query
    )
    dq_ref[:, :NOPE] = d_query[:, :NOPE].astype(jnp.bfloat16)
    dq_ref[:, NOPE:] = turned(d_query[:, NOPE:], cos_ref[...], -sin_ref[...]).astype(jnp.bfloat16)

    @pl.when(q_step == pl.num_programs(1) - 1)
    def _():
        dkv_ref[:, :NOPE] = dk_acc[:, :NOPE].astype(jnp.bfloat16)
        dkv_ref[:, NOPE:] = dv_acc[...].astype(jnp.bfloat16)

    @pl.when((q_step == pl.num_programs(1) - 1) & (head == pl.num_programs(0) - 1))
    def _():
        dkr_ref[...] = dk_acc[:, NOPE:].astype(jnp.bfloat16)


def attn_backward(my_ctx, query, keyval, kv_all, d_mixed, mixed, lse_rows, cosines, sines, scale):
    block_rows = query.shape[0]
    seq_len = keyval.shape[0]
    heads = query.shape[1] // 256
    grid_spec = pltpu.PrefetchScalarGridSpec(
        num_scalar_prefetch=1,
        grid=(heads, block_rows // KCHUNK),
        in_specs=[
            pl.BlockSpec((KCHUNK, 256), lambda h, i, c: (i, h)),
            pl.BlockSpec((seq_len, NOPE), lambda h, i, c: (0, 2 * h)),
            pl.BlockSpec((seq_len, 128), lambda h, i, c: (0, RANK // 128)),
            pl.BlockSpec((seq_len, VDIM), lambda h, i, c: (0, 2 * h + 1)),
            pl.BlockSpec((KCHUNK, VDIM), lambda h, i, c: (i, h)),
            pl.BlockSpec((KCHUNK, VDIM), lambda h, i, c: (i, h)),
            pl.BlockSpec((1, 1, KCHUNK), lambda h, i, c: (h, 0, i)),
            pl.BlockSpec((KCHUNK, 128), lambda h, i, c: (i, 0)),
            pl.BlockSpec((KCHUNK, 128), lambda h, i, c: (i, 0)),
        ],
        out_specs=[
            pl.BlockSpec((KCHUNK, 256), lambda h, i, c: (i, h)),
            pl.BlockSpec((seq_len, 256), lambda h, i, c: (0, h)),
            pl.BlockSpec((seq_len, 128), lambda h, i, c: (0, 0)),
        ],
        scratch_shapes=[
            pltpu.VMEM((seq_len, 256), jnp.float32),
            pltpu.VMEM((seq_len, VDIM), jnp.float32),
        ],
    )
    return pl.pallas_call(
        functools.partial(attn_bwd_kernel, scale=scale, block_rows=block_rows),
        grid_spec=grid_spec,
        out_shape=[
            jax.ShapeDtypeStruct((block_rows, heads * 256), jnp.bfloat16),
            jax.ShapeDtypeStruct((seq_len, heads * 256), jnp.bfloat16),
            jax.ShapeDtypeStruct((seq_len, 128), jnp.bfloat16),
        ],
        compiler_params=params(),
        cost_estimate=cost(9, 10),
        name="attn_backward",
    )(
        jnp.full((1,), my_ctx, jnp.int32),
        query, keyval, kv_all, keyval, d_mixed, mixed, lse_rows, cosines, sines,
    )


def resid_kernel(at_ref, x_ref, gain_ref, *refs, n_parts, n_slots):
    parts = refs[:n_parts]
    slots = refs[n_parts : n_parts + n_slots]
    hidden_ref, own_ref, acc_ref = refs[n_parts + n_slots :]
    blk = x_ref.shape[0]
    acc = x_ref[...].astype(jnp.float32)
    for k, slot in enumerate(slots):
        source = at_ref[k]
        weight = jnp.concatenate([part[source] for part in parts], 0)
        acc = acc + matmul(slot[...], weight)
    acc_ref[...] = acc
    hidden_ref[...] = (acc * rms_scale(acc) * gain_ref[...]).astype(jnp.bfloat16)
    own_start = at_ref[n_slots]

    @pl.when(pl.program_id(0) == own_start // blk)
    def _():
        own_ref[...] = acc_ref[pl.ds(pl.multiple_of(own_start % blk, ROWS), ROWS), :]


def resid_and_hidden(at, x, gain, parts, slots):
    rows = x.shape[0]
    blk = 512
    grid_spec = pltpu.PrefetchScalarGridSpec(
        num_scalar_prefetch=1,
        grid=(rows // blk,),
        in_specs=[pl.BlockSpec((blk, D), lambda i, a: (i, 0)), whole((1, D))]
        + [whole(part.shape) for part in parts]
        + [pl.BlockSpec((blk, slot.shape[1]), lambda i, a: (i, 0)) for slot in slots],
        out_specs=[pl.BlockSpec((blk, D), lambda i, a: (i, 0)), whole((ROWS, D))],
        scratch_shapes=[pltpu.VMEM((blk, D), jnp.float32)],
    )
    return pl.pallas_call(
        functools.partial(resid_kernel, n_parts=len(parts), n_slots=len(slots)),
        grid_spec=grid_spec,
        out_shape=[
            jax.ShapeDtypeStruct((rows, D), jnp.bfloat16),
            jax.ShapeDtypeStruct((ROWS, D), jnp.float32),
        ],
        compiler_params=params(),
        cost_estimate=cost(8.6, 24),
        name="resid_and_hidden",
    )(at, x, gain.reshape(1, D), *parts, *slots)


def strips(width):
    return [slice(at, min(at + 256, width)) for at in range(0, width, 256)]


def forward_kernel(x_ref, gate_w_ref, up_w_ref, act_ref, for_gate_ref, for_up_ref, gate_acc):
    phase = pl.program_id(1)

    @pl.when(phase == 0)
    def _():
        gate_acc[...] = matmul(x_ref[0], gate_w_ref[0])

    @pl.when(phase == 1)
    def _():
        for at in strips(gate_acc.shape[1]):
            up = matmul(x_ref[0], up_w_ref[0, :, at])
            silu, slope = silu_parts(gate_acc[:, at])
            act_ref[0, :, at] = (silu * up).astype(jnp.bfloat16)
            for_gate_ref[0, :, at] = (up * slope).astype(jnp.bfloat16)
            for_up_ref[0, :, at] = silu.astype(jnp.bfloat16)


def per_expert(shape):
    rest = (0,) * (len(shape) - 1)
    return pl.BlockSpec((1,) + shape[1:], lambda e, i: (e,) + rest)


def experts_forward(expert_in, gate, up):
    ff = gate.shape[2]
    hidden = jax.ShapeDtypeStruct((EXP_DEV, CAPB, ff), jnp.bfloat16)
    return pl.pallas_call(
        forward_kernel,
        grid=(EXP_DEV, 2),
        in_specs=[per_expert(expert_in.shape), per_expert(gate.shape), per_expert(up.shape)],
        out_specs=[per_expert(hidden.shape)] * 3,
        out_shape=[hidden] * 3,
        scratch_shapes=[pltpu.VMEM((CAPB, ff), jnp.float32)],
        compiler_params=params(),
        cost_estimate=cost(12, 36),
        name="experts_forward",
    )(expert_in, gate, up)


def backward_kernel(dout_ref, for_gate_ref, for_up_ref, down_ref, gate_ref, up_ref, both_ref, din_ref):
    phase = pl.program_id(1)
    ff = gate_ref.shape[2]

    @pl.when(phase == 0)
    def _():
        for at in strips(ff):
            d_act = times_transposed(dout_ref[0], down_ref[0, at, :])
            for_gate, for_up = for_gate_ref[0, :, at], for_up_ref[0, :, at]
            there = slice(ff + at.start, ff + at.stop)
            both_ref[0, :, at] = (d_act * for_gate.astype(jnp.float32)).astype(jnp.bfloat16)
            both_ref[0, :, there] = (d_act * for_up.astype(jnp.float32)).astype(jnp.bfloat16)

    @pl.when(phase > 0)
    def _():
        for at in strips(gate_ref.shape[1]):
            total = times_transposed(both_ref[0, :, :ff], gate_ref[0, at, :])
            total = total + times_transposed(both_ref[0, :, ff:], up_ref[0, at, :])
            din_ref[0, :, at] = total.astype(jnp.bfloat16)


def experts_backward(d_out, for_gate, for_up, gate, up, down):
    ff = gate.shape[2]
    cols = D // 2
    hidden = (EXP_DEV, CAPB, ff)
    both = (EXP_DEV, CAPB, 2 * ff)
    half_rows = pl.BlockSpec((1, cols, ff), lambda e, i: (e, jnp.maximum(i - 1, 0), 0))
    return pl.pallas_call(
        backward_kernel,
        grid=(EXP_DEV, 3),
        in_specs=[
            per_expert(d_out.shape), per_expert(hidden), per_expert(hidden),
            per_expert(down.shape), half_rows, half_rows,
        ],
        out_specs=[
            per_expert(both),
            pl.BlockSpec((1, CAPB, cols), lambda e, i: (e, 0, jnp.maximum(i - 1, 0))),
        ],
        out_shape=[
            jax.ShapeDtypeStruct(both, jnp.bfloat16),
            jax.ShapeDtypeStruct((EXP_DEV, CAPB, D), jnp.bfloat16),
        ],
        compiler_params=params(),
        cost_estimate=cost(18, 50),
        name="experts_backward",
    )(d_out, for_gate, for_up, down, gate, up)


def out_kernel(act_ref, mass_ref, down_ref, out_ref):
    out_ref[0] = (matmul(act_ref[0], down_ref[0]) * mass_ref[0]).astype(jnp.bfloat16)


def experts_out(act, mass, down):
    ff = act.shape[2]
    cols = D // 2
    return pl.pallas_call(
        out_kernel,
        grid=(EXP_DEV, 2),
        in_specs=[
            per_expert(act.shape), per_expert(mass.shape),
            pl.BlockSpec((1, ff, cols), lambda e, i: (e, 0, i)),
        ],
        out_specs=pl.BlockSpec((1, CAPB, cols), lambda e, i: (e, 0, i)),
        out_shape=jax.ShapeDtypeStruct((EXP_DEV, CAPB, D), jnp.bfloat16),
        compiler_params=params(),
        cost_estimate=cost(1, 4),
        name="experts_out",
    )(act, mass, down)


def products_kernel(*refs):
    out_ref = refs[-1]
    total = None
    for k in range(len(refs) // 2):
        product = matmul(refs[2 * k][...], refs[2 * k + 1][...])
        total = product if total is None else total + product
    out_ref[...] = total.astype(out_ref.dtype)


def sum_of_products(name, terms, gflop, mbytes):
    rows, blk = terms[0][0].shape[0], 512
    specs, flat = [], []
    for left, right in terms:
        specs += [whole(left.shape), pl.BlockSpec((right.shape[0], blk), lambda i: (0, i))]
        flat += [left, right]
    return pl.pallas_call(
        products_kernel,
        grid=(D // blk,),
        in_specs=specs,
        out_specs=pl.BlockSpec((rows, blk), lambda i: (0, i)),
        out_shape=jax.ShapeDtypeStruct((rows, D), jnp.bfloat16),
        compiler_params=params(),
        cost_estimate=cost(gflop / 5, mbytes / 5),
        name=name,
    )(*flat)


def shared_kernel(hidden_ref, dy_ref, gate_ref, up_ref, down_ref, act_ref, d_gate_ref, d_up_ref):
    hidden = hidden_ref[...]
    gate = times_transposed(hidden, gate_ref[...])
    up = times_transposed(hidden, up_ref[...])
    d_act = times_transposed(dy_ref[...], down_ref[...])
    silu, slope = silu_parts(gate)
    act_ref[...] = (silu * up).astype(jnp.bfloat16)
    d_gate_ref[...] = (d_act * up * slope).astype(jnp.bfloat16)
    d_up_ref[...] = (d_act * silu).astype(jnp.bfloat16)


def shared_experts(hidden_in, dy, gate, up, down):
    rows, blk = hidden_in.shape[0], 512
    width = down.shape[0]
    row_spec = lambda size: pl.BlockSpec((blk, size), lambda i: (i, 0))
    return pl.pallas_call(
        shared_kernel,
        grid=(rows // blk,),
        in_specs=[row_spec(D), row_spec(D)] + [whole(down.shape)] * 3,
        out_specs=[row_spec(width)] * 3,
        out_shape=[jax.ShapeDtypeStruct((rows, width), jnp.bfloat16)] * 3,
        compiler_params=params(),
        cost_estimate=cost(4.4, 15),
        name="shared_experts",
    )(hidden_in, dy, gate, up, down)


def parts_kernel(at_ref, *refs, n_terms):
    outs, total_ref = refs[2 * n_terms : -1], refs[-1]
    total = None
    for k in range(n_terms):
        product = matmul(refs[2 * k][...], refs[2 * k + 1][...])
        total = product if total is None else total + product
    total_ref[...] = total.astype(jnp.bfloat16)
    for k, out in enumerate(outs):
        out[...] = total_ref[pl.ds(pl.multiple_of(at_ref[k], ROWS), ROWS), :]


def row_parts(name, at, terms, gflop, mbytes):
    rows, blk = terms[0][0].shape[0], 512
    specs, flat = [], []
    for left, right in terms:
        specs += [
            pl.BlockSpec(left.shape, lambda i, a: (0, 0)),
            pl.BlockSpec((right.shape[0], blk), lambda i, a: (0, i)),
        ]
        flat += [left, right]
    grid_spec = pltpu.PrefetchScalarGridSpec(
        num_scalar_prefetch=1,
        grid=(D // blk,),
        in_specs=specs,
        out_specs=[pl.BlockSpec((ROWS, blk), lambda i, a: (0, i))] * (rows // ROWS),
        scratch_shapes=[pltpu.VMEM((rows, blk), jnp.bfloat16)],
    )
    return pl.pallas_call(
        functools.partial(parts_kernel, n_terms=len(terms)),
        grid_spec=grid_spec,
        out_shape=[jax.ShapeDtypeStruct((ROWS, D), jnp.bfloat16)] * (rows // ROWS),
        compiler_params=params(),
        cost_estimate=cost(gflop / 5, mbytes / 5),
        name=name,
    )(at, *flat)


def latent_kernel(at_ref, dkv_ref, kvw_ref, dkr_ref, *refs):
    outs, tile = refs[:-1], refs[-1]
    tile[:, :RANK] = times_transposed(dkv_ref[...], kvw_ref[...]).astype(jnp.bfloat16)
    tile[:, RANK:] = dkr_ref[...]
    for k, out in enumerate(outs):
        out[0] = tile[pl.ds(pl.multiple_of(at_ref[k], ROWS), ROWS), :]


def latent_parts(at, d_kv, keyval_weight, d_krope, n_ctx):
    blk = d_kv.shape[0] // n_ctx
    row_spec = lambda width: pl.BlockSpec((blk, width), lambda i, a: (i, 0))
    grid_spec = pltpu.PrefetchScalarGridSpec(
        num_scalar_prefetch=1,
        grid=(n_ctx,),
        in_specs=[
            row_spec(d_kv.shape[1]),
            pl.BlockSpec(keyval_weight.shape, lambda i, a: (0, 0)),
            row_spec(128),
        ],
        out_specs=[pl.BlockSpec((1, ROWS, RANK + 128), lambda i, a: (i, 0, 0))] * (blk // ROWS),
        scratch_shapes=[pltpu.VMEM((blk, RANK + 128), jnp.bfloat16)],
    )
    return pl.pallas_call(
        latent_kernel,
        grid_spec=grid_spec,
        out_shape=[jax.ShapeDtypeStruct((n_ctx, ROWS, RANK + 128), jnp.bfloat16)] * (blk // ROWS),
        compiler_params=params(),
        cost_estimate=cost(1, 6),
        name="latent_parts",
    )(at, d_kv, keyval_weight, d_krope)


def turn(values, axis, step):
    size = lax.axis_size(axis)
    return lax.ppermute(values, axis, [(i, (i + step) % size) for i in range(size)])


def move(values, flip):
    pairs = [(i, i ^ flip) for i in range(lax.axis_size("experts"))]
    return lax.ppermute(values, "experts", pairs)


def first_moves(values):
    return move(values, 4), move(values, 2), move(values, 1)


def last_moves(values, first):
    far, near, beside = first
    both = move(far, 2)
    return [values, beside, near, move(near, 1), far, move(far, 1), both, move(both, 1)]


def gather_slots(values):
    return last_moves(values, first_moves(values))


def scatter_sum(parts):
    def pair(k):
        return parts[k].astype(jnp.float32) + move(parts[k + 1], 1).astype(jnp.float32)

    def sent(values, flip):
        return move(values.astype(jnp.bfloat16), flip).astype(jnp.float32)

    both = sent(pair(6), 2)
    far = sent(pair(4) + both, 4)
    near = sent(pair(2), 2)
    return pair(0) + near + far


def butterfly(values, axis):
    size = lax.axis_size(axis)
    span = 1
    while span < size:
        pairs = [(i, i ^ span) for i in range(size)]
        values = values + lax.ppermute(values, axis, pairs)
        span *= 2
    return values


def gather_quarters(shard, dim):
    return lax.all_gather(shard, ("context", "dp"), axis=dim, tiled=True)


def tie(*values):
    return lax.optimization_barrier(values)


def grad_stages(product, split, dim):
    n_ctx, n_dp = lax.axis_size("context"), lax.axis_size("dp")
    my_ctx, my_dp = lax.axis_index("context"), lax.axis_index("dp")
    width = split.shape[2] // (n_ctx * n_dp)
    part = lambda c, d: lax.dynamic_slice_in_dim(split, (c * n_dp + d) * width, width, 2)
    got = []
    for j in range(1, n_dp):
        there = (my_dp + j) % n_dp
        sent = product(jnp.concatenate([part(c, there) for c in range(n_ctx)], 2), slice(None))
        got.append(turn(sent.astype(jnp.bfloat16), "dp", j))

    def near(c, experts):
        total = product(part(c, my_dp)[experts], experts)
        for other in got:
            total = total + lax.dynamic_slice_in_dim(other, c * width, width, dim)[
                experts
            ].astype(jnp.float32)
        return total.astype(jnp.bfloat16)

    sums = [
        [near((my_ctx + k) % n_ctx, slice(e, e + 1)) for k in range(1, n_ctx)]
        for e in range(EXP_DEV)
    ]
    return sums, lambda: near(my_ctx, slice(None))


def send_sums(sums):
    return [[turn(there, "context", k + 1) for k, there in enumerate(some)] for some in sums]


def finish_grad(heard, own):
    own = own.astype(jnp.float32)
    for others in zip(*heard):
        own = own + jnp.concatenate(others, 0).astype(jnp.float32)
    return own


def shared_finish_kernel(first_ref, own_ref, other_ref, gate_ref, up_ref, down_ref):
    width = gate_ref.shape[0]
    swapped = first_ref[0] > 0
    for k, out in enumerate((gate_ref, up_ref, down_ref)):
        own = own_ref[k * width : (k + 1) * width, :].astype(jnp.float32)
        other = other_ref[k * width : (k + 1) * width, :].astype(jnp.float32)
        half = own.shape[1]
        out[:, :half] = jnp.where(swapped, other, own)
        out[:, half:] = jnp.where(swapped, own, other)


def shared_finish(my_dp, own, other):
    rows, half = own.shape
    width = rows // 3
    half_spec = pl.BlockSpec((rows, half), lambda i, a: (0, 0))
    grid_spec = pltpu.PrefetchScalarGridSpec(
        num_scalar_prefetch=1,
        grid=(1,),
        in_specs=[half_spec, half_spec],
        out_specs=[pl.BlockSpec((width, 2 * half), lambda i, a: (0, 0))] * 3,
    )
    return pl.pallas_call(
        shared_finish_kernel,
        grid_spec=grid_spec,
        out_shape=[jax.ShapeDtypeStruct((width, 2 * half), jnp.float32)] * 3,
        compiler_params=params(),
        cost_estimate=cost(0, 13),
        name="shared_finish",
    )(jnp.full((1,), my_dp, jnp.int32), own, other)


def halves_sent(grad, dim):
    n_dp = lax.axis_size("dp")
    my_dp = lax.axis_index("dp")
    width = grad.shape[dim] // n_dp
    part = lambda j: lax.dynamic_slice_in_dim(grad, (my_dp + j) % n_dp * width, width, dim)
    heard = [turn(part(j).astype(jnp.bfloat16), "dp", j) for j in range(1, n_dp)]
    return part(0), heard


def halves_added(own, heard):
    for other in heard:
        own = own + other.astype(jnp.float32)
    return own.astype(jnp.bfloat16)


def context_sent(own):
    return turn(own, "context", 1) if lax.axis_size("context") == 2 else lax.psum(own, "context")


def context_added(own, heard):
    if lax.axis_size("context") != 2:
        return heard
    return (own.astype(jnp.float32) + heard.astype(jnp.float32)).astype(jnp.bfloat16)


def halves_joined(own, dim):
    n_dp = lax.axis_size("dp")
    my_dp = lax.axis_index("dp")
    shape = list(own.shape)
    width = shape[dim]
    shape[dim] = width * n_dp
    total = jnp.zeros(shape, jnp.bfloat16)
    for j in range(n_dp):
        piece = turn(own, "dp", j) if j else own
        at = (my_dp + n_dp - j) % n_dp
        total = lax.dynamic_update_slice_in_dim(total, piece, at * width, dim)
    return total.astype(jnp.float32)


def local(
    layer_input,
    routes,
    route_weights,
    query_weight,
    latent_weight,
    keyval_weight,
    output_weight,
    attn_gain,
    latent_gain,
    ffn_gain,
    shared_gate,
    shared_up,
    shared_down,
    expert_gate,
    expert_up,
    expert_down,
    cotangent,
):
    n_exp = lax.axis_size("experts")
    n_ctx = lax.axis_size("context")
    n_dp = lax.axis_size("dp")
    my_exp = lax.axis_index("experts")
    my_ctx = lax.axis_index("context")
    my_dp = lax.axis_index("dp")
    block_rows = layer_input.shape[2]
    heads_dev = query_weight.shape[1] // (NOPE + ROPE)
    scale = (NOPE + ROPE) ** (-0.5)
    low = jnp.bfloat16
    route_ids = routes.reshape(block_rows, TOPK)
    route_mass = route_weights.reshape(block_rows, TOPK)
    grad_out = cotangent.reshape(block_rows, D)
    own_start = my_exp * ROWS

    def own_rows(values):
        return lax.dynamic_slice_in_dim(values, own_start, ROWS, 0)

    full_gate = gather_quarters(expert_gate, 1)
    full_up = gather_quarters(expert_up, 1)
    full_down = gather_quarters(expert_down, 2)
    lane = jnp.arange(128, dtype=jnp.int32)[None, :]
    freqs = ROPE_BASE ** (-(lane % (ROPE // 2)).astype(jnp.float32) * 2.0 / ROPE)

    def tables(positions):
        turns = positions.astype(jnp.float32)[:, None] * freqs
        sines = jnp.sin(turns)
        sines = jnp.where(lane < ROPE // 2, -sines, sines)
        return (jnp.where(lane < ROPE, jnp.cos(turns), 0.0), jnp.where(lane < ROPE, sines, 0.0))

    query_pos = my_ctx * block_rows + jnp.arange(block_rows, dtype=jnp.int32)
    cos_q, sin_q = tables(query_pos)
    x_block = layer_input.reshape(block_rows, D)
    latent_turned = latent_weight.T
    ow_rows = output_weight.shape[0] // n_dp
    ow_mine = lax.dynamic_slice_in_dim(output_weight, my_dp * ow_rows, ow_rows, 0)
    ow_first = first_moves(ow_mine)
    normed, query, kv_low = front(
        x_block, attn_gain, query_weight, latent_turned, latent_gain, cos_q, sin_q
    )
    kv_low, ow_first = lax.optimization_barrier((kv_low, ow_first))
    ow_slots = last_moves(ow_mine, ow_first)
    kv_all = jnp.zeros((n_ctx * block_rows, RANK + 128), low)
    kv_all = lax.dynamic_update_slice_in_dim(kv_all, kv_low, 0, 0)
    kv_own = own_rows(kv_low)
    kv_heard = []
    for k in range(1, n_ctx):
        pairs = [(i, i + k) for i in range(n_ctx - k)]
        kv_heard.append(lax.ppermute(kv_own, "context", pairs))
    if kv_heard:
        for k, rows in enumerate(gather_slots(jnp.stack(kv_heard))):
            for j in range(n_ctx - 1):
                at = (j + 1) * block_rows + (my_exp ^ k) * ROWS
                kv_all = lax.dynamic_update_slice_in_dim(kv_all, rows[j], at, 0)
    latent_all = kv_all[:, :RANK]
    expanded = matmul(latent_all, keyval_weight).astype(low)
    mixed, logsums = attn_forward(my_ctx, query, expanded, kv_all, scale)

    def head_turn(values, back):
        step = my_dp * VDIM * (heads_dev // n_dp)
        width = values.shape[1]
        twice = jnp.concatenate([values, values], 1)
        start = (width - step) % width if back else step
        return lax.dynamic_slice_in_dim(twice, start, width, 1)

    mixed_turned = head_turn(mixed, False)
    mixed_first = first_moves(mixed_turned)
    mixed_first, ow_slots = lax.optimization_barrier((mixed_first, ow_slots))
    ow_near = jnp.zeros((n_exp, ow_rows, D), low)
    for k, rows in enumerate(ow_slots):
        ow_near = lax.dynamic_update_slice_in_dim(ow_near, rows[None], my_exp ^ k, 0)
    ow_parts = [turn(ow_near, "dp", j) if j else ow_near for j in range(n_dp)]
    mixed_slots = last_moves(mixed_turned, mixed_first)
    slot_at = jnp.stack([my_exp ^ k for k in range(n_exp)] + [own_start]).astype(jnp.int32)
    hidden_in, resid_own = resid_and_hidden(slot_at, x_block, ffn_gain, ow_parts, mixed_slots)
    scale_mid_own = rms_scale(resid_own)

    expert_ids = my_exp * EXP_DEV + jnp.arange(EXP_DEV, dtype=jnp.int32)
    chosen = route_ids[:, :, None] == expert_ids[None, None, :]
    member = jnp.any(chosen, 1)
    mass = jnp.sum(jnp.where(chosen, route_mass[:, :, None], 0.0), 1)
    earlier = (
        jnp.arange(block_rows, dtype=jnp.int32)[:, None]
        > jnp.arange(block_rows, dtype=jnp.int32)[None, :]
    ).astype(low)
    rank = matmul(earlier, member.astype(low)).astype(jnp.int32)
    slot_of = jnp.where(member, rank, -1).T
    taken = slot_of[:, None, :] == jnp.arange(CAPB, dtype=jnp.int32)[None, :, None]
    slot_mass = jnp.sum(jnp.where(taken, mass.T[:, None, :], 0.0), -1)
    pick = taken.astype(low).reshape(EXP_DEV * CAPB, block_rows)
    spread = (
        jnp.where(member, rank, -1)[:, :, None] == jnp.arange(CAPB, dtype=jnp.int32)[None, None, :]
    ).astype(low).reshape(block_rows, EXP_DEV * CAPB)

    d_out = (
        (matmul(pick, grad_out) * slot_mass.reshape(-1, 1)).astype(low).reshape(EXP_DEV, CAPB, D)
    )
    expert_in = matmul(pick, hidden_in).astype(low).reshape(EXP_DEV, CAPB, D)
    act_e, for_gate, for_up = experts_forward(expert_in, full_gate, full_up)
    act_s, d_gate_s, d_up_s = shared_experts(
        hidden_in, grad_out, shared_gate.T, shared_up.T, shared_down
    )
    pool = {}

    def point(name, *carriers):
        extra = {key: value for key, value in pool.items() if PLACES.get(key) == name}
        carriers, extra = lax.optimization_barrier((carriers, extra))
        pool.update(extra)
        return carriers if len(carriers) > 1 else carriers[0]

    slots_all = EXP_DEV * CAPB
    target_rows = jnp.stack([(my_exp ^ k) * ROWS for k in range(n_exp)]).astype(jnp.int32)

    def reduce_rows(name, terms, gflop, mbytes):
        if OFFLOAD[name]:
            return [sum_of_products(name, terms, gflop, mbytes)]
        return list(row_parts(name, target_rows, terms, gflop, mbytes))

    def reduced(parts):
        if len(parts) > 1:
            return scatter_sum(parts)
        return lax.psum_scatter(parts[0], "experts", scatter_dimension=0, tiled=True)

    down_sums, down_rest = grad_stages(
        lambda part, some: jnp.einsum(
            "ecf,ecd->efd", act_e[some], part, preferred_element_type=jnp.float32
        ),
        d_out,
        2,
    )
    d_out, down_sums, act_s = point("back", d_out, down_sums, act_s)
    pool["down0"], pool["down1"] = send_sums(down_sums)
    d_both, d_in_e = experts_backward(d_out, for_gate, for_up, full_gate, full_up, full_down)
    spread = point("spread", spread)
    d_hidden_parts = reduce_rows(
        "d_hidden",
        [
            (d_gate_s, shared_gate.T),
            (d_up_s, shared_up.T),
            (spread, d_in_e.reshape(slots_all, D)),
        ],
        7.3, 16,
    )
    expert_in, d_both, d_hidden_parts = point("both", expert_in, d_both, d_hidden_parts)
    d_hidden_own = reduced(d_hidden_parts)
    both_sums, both_rest = grad_stages(
        lambda part, some: jnp.einsum(
            "ecd,ecf->edf", part, d_both[some], preferred_element_type=jnp.float32
        ),
        expert_in,
        1,
    )
    act_e, both_sums = point("act", act_e, both_sums)
    pool["both0"], pool["both1"] = send_sums(both_sums)
    pool["down_own"], pool["both_own"] = down_rest(), both_rest()
    out_e = experts_out(act_e, slot_mass[:, :, None], full_down)
    d_shared = jnp.concatenate([d_gate_s, d_up_s], 1)
    shared_grads = jnp.concatenate(
        [contract_rows(d_shared, hidden_in), contract_rows(act_s, grad_out)], 0
    )
    pool["shared_own"] = halves_added(*halves_sent(shared_grads, 1))
    out_e = point("ffn", out_e)
    ffn_parts = reduce_rows(
        "ffn_part",
        [(act_s, shared_down), (spread, out_e.reshape(slots_all, D))],
        5.8, 14,
    )
    d_hidden_own, ffn_parts = point("hid", d_hidden_own, ffn_parts)
    pool["ffn_out"] = reduced(ffn_parts)
    d_hidden_own = d_hidden_own.astype(jnp.float32)
    grad_own = own_rows(grad_out).astype(jnp.float32)

    def norm_mid(values_in):
        return values_in * rms_scale(values_in) * ffn_gain

    _, mid_pull = jax.vjp(norm_mid, resid_own)
    d_resid_own = grad_own + mid_pull(d_hidden_own)[0]
    d_ffn_gain = jnp.sum(d_hidden_own * resid_own * scale_mid_own, 0)
    d_resid_low = point("resid", d_resid_own.astype(low))

    d_mixed_parts = [
        times_transposed(d_resid_low, part.reshape(-1, D))
        .astype(low)
        .reshape(ROWS, n_exp, -1)
        .transpose(1, 0, 2)
        for part in ow_parts
    ]
    d_mixed = lax.all_to_all(jnp.concatenate(d_mixed_parts, 2), "experts", 0, 0, tiled=True)
    if OFFLOAD["d_resid"]:
        pool["d_resid"] = lax.all_gather(d_resid_low, "experts", axis=0, tiled=True)
    else:
        pool["d_resid"] = gather_slots(d_resid_low)
    d_mixed = point("mix", d_mixed)
    pool["shared_heard"] = context_sent(pool["shared_own"])
    d_mixed = head_turn(d_mixed.reshape(block_rows, heads_dev * VDIM), True)

    d_query, d_kv, d_krope = attn_backward(
        my_ctx, query, expanded, kv_all, d_mixed, mixed, logsums, cos_q, sin_q, scale
    )
    d_kv = point("kv", d_kv)
    lat_parts = list(latent_parts(target_rows, d_kv, keyval_weight, d_krope, n_ctx))
    head_width = NOPE + ROPE
    d_query_low = jnp.concatenate(
        [d_query[:, 256 * h : 256 * h + head_width] for h in range(heads_dev)], 1
    )
    d_query_low, lat_parts[0] = point("query", d_query_low, lat_parts[0])
    if OFFLOAD["d_norm"]:
        d_norm_part = times_transposed(d_query_low, query_weight).astype(low)
        pool["d_norm"] = lax.psum_scatter(
            d_norm_part, "experts", scatter_dimension=0, tiled=True
        )
    else:
        parts = row_parts("d_norm", target_rows, [(d_query_low, query_weight.T)], 1.6, 8)
        pool["d_norm"] = scatter_sum(parts)
    d_lat_blocks = point("lat", scatter_sum(lat_parts))
    d_comp_own = d_lat_blocks[0]
    for k in range(1, n_ctx):
        pairs = [(i, i - k) for i in range(k, n_ctx)]
        d_comp_own = d_comp_own + lax.ppermute(
            d_lat_blocks[k].astype(low), "context", pairs
        ).astype(jnp.float32)

    own_pos = my_ctx * block_rows + own_start + jnp.arange(ROWS, dtype=jnp.int32)
    cos_k, sin_k = angles(own_pos)
    own_normed = own_rows(normed)

    def latent_fn(comp_rows, lat_gain):
        lat_part = comp_rows[:, :RANK] * rms_scale(comp_rows[:, :RANK]) * lat_gain
        return jnp.concatenate([lat_part, rotate(comp_rows[:, RANK:], cos_k, sin_k)], -1)

    _, kv_pull = jax.vjp(latent_fn, matmul(own_normed, latent_weight), latent_gain)
    d_comp, d_lat_gain = kv_pull(d_comp_own[:, : RANK + ROPE])
    d_comp_low = point("comp", d_comp.astype(low))
    d_norm_own = pool["d_norm"].astype(jnp.float32)
    d_norm_total = d_norm_own + times_transposed(d_comp_low, latent_weight)

    def norm_in(values_in, gain_in):
        return values_in * rms_scale(values_in) * gain_in

    _, in_pull = jax.vjp(norm_in, own_rows(x_block).astype(jnp.float32), attn_gain)
    d_in_rows, d_attn_gain = in_pull(d_norm_total)
    input_grad = (d_resid_own + d_in_rows).reshape(1, 1, ROWS, D)


    ff = expert_gate.shape[2]
    both_own, both_heard = pool["both_own"], [pool["both0"], pool["both1"]]
    gate_heard = [[v[:, :, :ff] for v in some] for some in both_heard]
    up_heard = [[v[:, :, ff:] for v in some] for some in both_heard]
    expert_gate_grad = finish_grad(gate_heard, both_own[:, :, :ff])
    expert_up_grad = finish_grad(up_heard, both_own[:, :, ff:])
    expert_down_grad = finish_grad([pool["down0"], pool["down1"]], pool["down_own"])
    layer_output = (resid_own + pool["ffn_out"].astype(jnp.float32)).astype(low)
    layer_output = layer_output.reshape(1, 1, ROWS, D)

    shared_own = context_added(pool["shared_own"], pool["shared_heard"])
    shared_gate_grad, shared_up_grad, shared_down_grad = shared_finish(
        my_dp, shared_own, turn(shared_own, "dp", 1)
    )
    shared_gate_grad, shared_up_grad = shared_gate_grad.T, shared_up_grad.T

    def weight_grad(product):
        own = halves_added(*halves_sent(product, 0))
        return halves_joined(context_added(own, context_sent(own)), 0)

    query_grad = weight_grad(contract_rows(normed, d_query_low))
    keyval_grad = weight_grad(contract_rows(latent_all, d_kv))
    d_resid_block = pool["d_resid"]
    if not OFFLOAD["d_resid"]:
        slots, d_resid_block = d_resid_block, jnp.zeros((block_rows, D), low)
        for k, rows in enumerate(slots):
            d_resid_block = lax.dynamic_update_slice_in_dim(
                d_resid_block, rows, (my_exp ^ k) * ROWS, 0
            )
    output_grad = weight_grad(contract_rows(mixed, d_resid_block))

    grad_latent = contract_rows(d_comp_low, own_normed)
    lat_half_cols = D // n_dp
    lat_cols = lat_half_cols // n_exp

    def columns(values, at, width):
        return lax.dynamic_slice_in_dim(values, at, width, 1)

    lat_half = columns(grad_latent, my_dp * lat_half_cols, lat_half_cols)
    for j in range(1, n_dp):
        sent = columns(grad_latent, (my_dp + j) % n_dp * lat_half_cols, lat_half_cols)
        lat_half = lat_half + turn(sent.astype(low), "dp", j).astype(jnp.float32)
    lat_half = lat_half.astype(low)
    lat_own = scatter_sum([columns(lat_half, (my_exp ^ k) * lat_cols, lat_cols) for k in range(n_exp)])
    lat_own = point("lat_own", butterfly(lat_own, "context").astype(low))
    lat_half = jnp.zeros((RANK + ROPE, lat_half_cols), low)
    for k, part in enumerate(gather_slots(lat_own)):
        lat_half = lax.dynamic_update_slice_in_dim(lat_half, part, (my_exp ^ k) * lat_cols, 1)
    latent_grad = jnp.zeros((RANK + ROPE, D), low)
    for j in range(n_dp):
        piece = turn(lat_half, "dp", j) if j else lat_half
        at = (my_dp + n_dp - j) % n_dp
        latent_grad = lax.dynamic_update_slice_in_dim(latent_grad, piece, at * lat_half_cols, 1)
    latent_grad = latent_grad.astype(jnp.float32).T

    gains = jnp.concatenate([d_attn_gain, d_lat_gain, d_ffn_gain])
    for axis in ("dp", "context", "experts"):
        gains = butterfly(gains, axis)
    attn_gain_grad = gains[:D]
    latent_gain_grad = gains[D : D + RANK]
    ffn_gain_grad = gains[D + RANK :]
    return (
        layer_output,
        input_grad,
        query_grad,
        latent_grad,
        keyval_grad,
        output_grad,
        attn_gain_grad,
        latent_gain_grad,
        ffn_gain_grad,
        shared_gate_grad,
        shared_up_grad,
        shared_down_grad,
        expert_gate_grad,
        expert_up_grad,
        expert_down_grad,
    )


def solution(mesh):
    in_specs = (
        P("dp", "context", None, None),
        P("dp", "context", None, None),
        P("dp", "context", None, None),
        P(None, "experts"),
        P(),
        P(None, "experts"),
        P("experts", None),
        P(),
        P(),
        P(),
        P(None, "experts"),
        P(None, "experts"),
        P("experts", None),
        P("experts", ("context", "dp"), None),
        P("experts", ("context", "dp"), None),
        P("experts", None, ("context", "dp")),
        P("dp", "context", None, None),
    )
    out_specs = (
        P("dp", "context", "experts", None),
        P("dp", "context", "experts", None),
        P(None, "experts"),
        P(),
        P(None, "experts"),
        P("experts", None),
        P(),
        P(),
        P(),
        P(None, "experts"),
        P(None, "experts"),
        P("experts", None),
        P("experts", ("context", "dp"), None),
        P("experts", ("context", "dp"), None),
        P("experts", None, ("context", "dp")),
    )
    return jax.shard_map(local, mesh=mesh, in_specs=in_specs, out_specs=out_specs, check_vma=False)
```

```python
import functools

import jax
import jax.numpy as jnp
from jax import lax
from jax.experimental import pallas as pl
from jax.experimental.pallas import tpu as pltpu
from jax.sharding import PartitionSpec as P

D = 2048
NOPE = 128
ROPE = 64
VDIM = 128
RANK = 512
TOPK = 6
EXP_DEV = 2
ROWS = 128
CAPB = 512


EPSILON = 1e-06
ROPE_BASE = 50000.0
MASKED = -1e30


def angles(positions):
    half_width = ROPE // 2
    freqs_table = ROPE_BASE ** (-jnp.arange(half_width, dtype=jnp.float32) * 2.0 / ROPE)
    turned = positions.astype(jnp.float32)[:, None] * freqs_table[None, :]
    return (jnp.cos(turned), jnp.sin(turned))


def rotate(values_in, cosines, sines):
    half_width = values_in.shape[-1] // 2
    first_half = values_in[..., :half_width]
    second_half = values_in[..., half_width:]
    return jnp.concatenate(
        [first_half * cosines - second_half * sines, second_half * cosines + first_half * sines], -1
    )


def rms_scale(values_in):
    return lax.rsqrt(jnp.mean(values_in * values_in, -1, keepdims=True) + EPSILON)


def matmul(left_side, right_side):
    return jnp.dot(left_side, right_side, preferred_element_type=jnp.float32)


def contract_rows(left_side, right_side):
    return lax.dot_general(
        left_side, right_side, (((0,), (0,)), ((), ())), preferred_element_type=jnp.float32
    )


def times_transposed(left_side, right_side):
    return lax.dot_general(
        left_side, right_side, (((1,), (1,)), ((), ())), preferred_element_type=jnp.float32
    )


def silu_parts(gate_vals):
    sigmoid_g = jax.nn.sigmoid(gate_vals)
    return (gate_vals * sigmoid_g, sigmoid_g * (1.0 + gate_vals * (1.0 - sigmoid_g)))


OFFLOAD = {"d_hidden": True, "ffn_part": False, "d_norm": True, "d_resid": True}
PLACES = {"down0": "spread", "down1": "act", "both0": "mix", "both1": "lat_own", "down_own": "mix", "both_own": "ffn", "shared_own": "ffn", "shared_heard": "comp", "d_norm": "lat_own"}
KCHUNK = 512
VMEM_LIMIT = 56 * 2**20


def params():
    return pltpu.CompilerParams(vmem_limit_bytes=VMEM_LIMIT)


def cost(gflop, mbytes):
    return pl.CostEstimate(
        flops=int(gflop * 1e9), bytes_accessed=int(mbytes * 1e6), transcendentals=0
    )


def whole(shape):
    zeros = (0,) * len(shape)
    return pl.BlockSpec(shape, lambda *at: zeros)


def turned(tile, cosines, sines):
    lane = lax.broadcasted_iota(jnp.int32, tile.shape, 1)
    half_width = ROPE // 2
    other = jnp.where(
        lane < half_width, pltpu.roll(tile, 128 - half_width, 1), pltpu.roll(tile, half_width, 1)
    )
    return tile * cosines + other * sines


def front_kernel(x_ref, gain_ref, wq_ref, wl_ref, lgain_ref, cos_ref, sin_ref, normed_ref, q_ref, kv_ref):
    x = x_ref[...].astype(jnp.float32)
    normed = (x * rms_scale(x) * gain_ref[...]).astype(jnp.bfloat16)
    normed_ref[...] = normed
    cosines, sines = cos_ref[...], sin_ref[...]
    low_part = times_transposed(normed, wl_ref[:RANK, :])
    kv_ref[:, :RANK] = (low_part * rms_scale(low_part) * lgain_ref[...]).astype(jnp.bfloat16)
    rope_rows = jnp.concatenate([wl_ref[RANK:, :], jnp.zeros((128 - ROPE, D), jnp.bfloat16)], 0)
    rope_part = times_transposed(normed, rope_rows)
    kv_ref[:, RANK:] = turned(rope_part, cosines, sines).astype(jnp.bfloat16)
    raw = matmul(normed, wq_ref[...])
    width = raw.shape[1]
    for head in range(width // (NOPE + ROPE)):
        start = head * (NOPE + ROPE)
        here = pltpu.roll(raw, width - start, 1) if start else raw
        q_ref[:, head * 256 : head * 256 + NOPE] = here[:, :NOPE].astype(jnp.bfloat16)
        q_ref[:, head * 256 + NOPE : head * 256 + 256] = turned(
            here[:, NOPE : NOPE + 128], cosines, sines
        ).astype(jnp.bfloat16)


def front(x, gain, query_weight, latent_turned, lat_gain, cosines, sines):
    rows = x.shape[0]
    blk = 512
    heads = query_weight.shape[1] // (NOPE + ROPE)
    row_spec = lambda width: pl.BlockSpec((blk, width), lambda i: (i, 0))
    return pl.pallas_call(
        front_kernel,
        grid=(rows // blk,),
        in_specs=[
            row_spec(D), whole((1, D)), whole(query_weight.shape), whole(latent_turned.shape),
            whole((1, RANK)), row_spec(128), row_spec(128),
        ],
        out_specs=[row_spec(D), row_spec(heads * 256), row_spec(RANK + 128)],
        out_shape=[
            jax.ShapeDtypeStruct((rows, D), jnp.bfloat16),
            jax.ShapeDtypeStruct((rows, heads * 256), jnp.bfloat16),
            jax.ShapeDtypeStruct((rows, RANK + 128), jnp.bfloat16),
        ],
        compiler_params=params(),
        cost_estimate=cost(4.5, 16),
        name="front",
    )(x, gain.reshape(1, D), query_weight, latent_turned, lat_gain.reshape(1, RANK), cosines, sines)


def to_row(column_tile):
    ones = jnp.ones((8, 128), jnp.float32)
    return lax.dot_general(
        ones, column_tile, (((1,), (1,)), ((), ())),
        precision=lax.Precision.HIGHEST, preferred_element_type=jnp.float32,
    )[0:1]


def attn_fwd_kernel(ctx_ref, q_ref, kn_ref, kr_ref, v_ref, out_ref, lse_ref, *, scale, block_rows):
    q_step = pl.program_id(1)
    rows = q_ref.shape[0]
    query = q_ref[...]

    def step(chunk, carry, masked):
        row_max, denom, acc = carry
        at = pl.ds(pl.multiple_of(chunk * KCHUNK, KCHUNK), KCHUNK)
        keys = jnp.concatenate([kn_ref[at, :], kr_ref[at, :]], -1)
        scores = times_transposed(query, keys) * scale
        if masked:
            row_at = lax.broadcasted_iota(jnp.int32, scores.shape, 0)
            col_at = lax.broadcasted_iota(jnp.int32, scores.shape, 1)
            scores = jnp.where(col_at <= row_at, scores, MASKED)
        new_max = jnp.maximum(row_max, jnp.max(scores, -1, keepdims=True))
        shrink = jnp.exp(row_max - new_max)
        terms = jnp.exp(scores - new_max)
        denom = denom * shrink + jnp.sum(terms, -1, keepdims=True)
        acc = acc * shrink + matmul(terms.astype(jnp.bfloat16), v_ref[at, :])
        return new_max, denom, acc

    carry = (
        jnp.full((rows, 1), MASKED, jnp.float32),
        jnp.zeros((rows, 1), jnp.float32),
        jnp.zeros((rows, VDIM), jnp.float32),
    )
    carry = step(q_step, carry, True)
    carry = lax.fori_loop(0, q_step, lambda i, c: step(i, c, False), carry)
    per_block = block_rows // KCHUNK
    carry = lax.fori_loop(
        per_block, per_block * (1 + ctx_ref[0]), lambda i, c: step(i, c, False), carry
    )
    row_max, denom, acc = carry
    out_ref[...] = (acc / denom).astype(jnp.bfloat16)
    lane = lax.broadcasted_iota(jnp.int32, (rows, 128), 1)
    lse_ref[0] = to_row(jnp.where(lane == 0, row_max + jnp.log(denom), 0.0))


def attn_forward(my_ctx, query, keyval, kv_all, scale):
    block_rows = query.shape[0]
    seq_len = keyval.shape[0]
    heads = query.shape[1] // 256
    grid_spec = pltpu.PrefetchScalarGridSpec(
        num_scalar_prefetch=1,
        grid=(heads, block_rows // KCHUNK),
        in_specs=[
            pl.BlockSpec((KCHUNK, 256), lambda h, i, c: (i, h)),
            pl.BlockSpec((seq_len, NOPE), lambda h, i, c: (0, 2 * h)),
            pl.BlockSpec((seq_len, 128), lambda h, i, c: (0, RANK // 128)),
            pl.BlockSpec((seq_len, VDIM), lambda h, i, c: (0, 2 * h + 1)),
        ],
        out_specs=[
            pl.BlockSpec((KCHUNK, VDIM), lambda h, i, c: (i, h)),
            pl.BlockSpec((1, 1, KCHUNK), lambda h, i, c: (h, 0, i)),
        ],
    )
    return pl.pallas_call(
        functools.partial(attn_fwd_kernel, scale=scale, block_rows=block_rows),
        grid_spec=grid_spec,
        out_shape=[
            jax.ShapeDtypeStruct((block_rows, heads * VDIM), jnp.bfloat16),
            jax.ShapeDtypeStruct((heads, 1, block_rows), jnp.float32),
        ],
        compiler_params=params(),
        cost_estimate=cost(4, 8),
        name="attn_forward",
    )(jnp.full((1,), my_ctx, jnp.int32), query, keyval, kv_all, keyval)


def attn_bwd_kernel(
    ctx_ref, q_ref, kn_ref, kr_ref, v_ref, dmix_ref, mix_ref, lse_ref, cos_ref, sin_ref,
    dq_ref, dkv_ref, dkr_ref, dk_acc, dv_acc, *, scale, block_rows,
):
    head = pl.program_id(0)
    q_step = pl.program_id(1)
    rows = q_ref.shape[0]

    @pl.when(q_step == 0)
    def _():
        dv_acc[...] = jnp.zeros_like(dv_acc)
        dk_acc[:, :NOPE] = jnp.zeros((dk_acc.shape[0], NOPE), jnp.float32)

    @pl.when((q_step == 0) & (head == 0))
    def _():
        dk_acc[:, NOPE:] = jnp.zeros((dk_acc.shape[0], 128), jnp.float32)

    query = q_ref[...]
    dmix = dmix_ref[...]
    lse = lse_ref[0]
    delta = to_row(dmix.astype(jnp.float32) * mix_ref[...].astype(jnp.float32))

    def step(chunk, d_query, masked):
        at = pl.ds(pl.multiple_of(chunk * KCHUNK, KCHUNK), KCHUNK)
        keys = jnp.concatenate([kn_ref[at, :], kr_ref[at, :]], -1)
        scores = times_transposed(keys, query) * scale - lse
        if masked:
            key_at = lax.broadcasted_iota(jnp.int32, scores.shape, 0)
            row_at = lax.broadcasted_iota(jnp.int32, scores.shape, 1)
            scores = jnp.where(key_at <= row_at, scores, MASKED)
        probs = jnp.exp(scores)
        dprob = times_transposed(v_ref[at, :], dmix)
        d_raw = (probs * (dprob - delta) * scale).astype(jnp.bfloat16)
        dv_acc[at, :] += matmul(probs.astype(jnp.bfloat16), dmix)
        dk_acc[at, :] += matmul(d_raw, query)
        return d_query + contract_rows(d_raw, keys)

    d_query = step(q_step, jnp.zeros((rows, 256), jnp.float32), True)
    d_query = lax.fori_loop(0, q_step, lambda i, c: step(i, c, False), d_query)
    per_block = block_rows // KCHUNK
    d_query = lax.fori_loop(
        per_block, per_block * (1 + ctx_ref[0]), lambda i, c: step(i, c, False), d_query
    )
    dq_ref[:, :NOPE] = d_query[:, :NOPE].astype(jnp.bfloat16)
    dq_ref[:, NOPE:] = turned(d_query[:, NOPE:], cos_ref[...], -sin_ref[...]).astype(jnp.bfloat16)

    @pl.when(q_step == pl.num_programs(1) - 1)
    def _():
        dkv_ref[:, :NOPE] = dk_acc[:, :NOPE].astype(jnp.bfloat16)
        dkv_ref[:, NOPE:] = dv_acc[...].astype(jnp.bfloat16)

    @pl.when((q_step == pl.num_programs(1) - 1) & (head == pl.num_programs(0) - 1))
    def _():
        dkr_ref[...] = dk_acc[:, NOPE:].astype(jnp.bfloat16)


def attn_backward(my_ctx, query, keyval, kv_all, d_mixed, mixed, lse_rows, cosines, sines, scale):
    block_rows = query.shape[0]
    seq_len = keyval.shape[0]
    heads = query.shape[1] // 256
    grid_spec = pltpu.PrefetchScalarGridSpec(
        num_scalar_prefetch=1,
        grid=(heads, block_rows // KCHUNK),
        in_specs=[
            pl.BlockSpec((KCHUNK, 256), lambda h, i, c: (i, h)),
            pl.BlockSpec((seq_len, NOPE), lambda h, i, c: (0, 2 * h)),
            pl.BlockSpec((seq_len, 128), lambda h, i, c: (0, RANK // 128)),
            pl.BlockSpec((seq_len, VDIM), lambda h, i, c: (0, 2 * h + 1)),
            pl.BlockSpec((KCHUNK, VDIM), lambda h, i, c: (i, h)),
            pl.BlockSpec((KCHUNK, VDIM), lambda h, i, c: (i, h)),
            pl.BlockSpec((1, 1, KCHUNK), lambda h, i, c: (h, 0, i)),
            pl.BlockSpec((KCHUNK, 128), lambda h, i, c: (i, 0)),
            pl.BlockSpec((KCHUNK, 128), lambda h, i, c: (i, 0)),
        ],
        out_specs=[
            pl.BlockSpec((KCHUNK, 256), lambda h, i, c: (i, h)),
            pl.BlockSpec((seq_len, 256), lambda h, i, c: (0, h)),
            pl.BlockSpec((seq_len, 128), lambda h, i, c: (0, 0)),
        ],
        scratch_shapes=[
            pltpu.VMEM((seq_len, 256), jnp.float32),
            pltpu.VMEM((seq_len, VDIM), jnp.float32),
        ],
    )
    return pl.pallas_call(
        functools.partial(attn_bwd_kernel, scale=scale, block_rows=block_rows),
        grid_spec=grid_spec,
        out_shape=[
            jax.ShapeDtypeStruct((block_rows, heads * 256), jnp.bfloat16),
            jax.ShapeDtypeStruct((seq_len, heads * 256), jnp.bfloat16),
            jax.ShapeDtypeStruct((seq_len, 128), jnp.bfloat16),
        ],
        compiler_params=params(),
        cost_estimate=cost(9, 10),
        name="attn_backward",
    )(
        jnp.full((1,), my_ctx, jnp.int32),
        query, keyval, kv_all, keyval, d_mixed, mixed, lse_rows, cosines, sines,
    )


def resid_kernel(at_ref, x_ref, gain_ref, *refs, n_parts, n_slots):
    parts = refs[:n_parts]
    slots = refs[n_parts : n_parts + n_slots]
    hidden_ref, own_ref, acc_ref = refs[n_parts + n_slots :]
    blk = x_ref.shape[0]
    acc = x_ref[...].astype(jnp.float32)
    for k, slot in enumerate(slots):
        source = at_ref[k]
        weight = jnp.concatenate([part[source] for part in parts], 0)
        acc = acc + matmul(slot[...], weight)
    acc_ref[...] = acc
    hidden_ref[...] = (acc * rms_scale(acc) * gain_ref[...]).astype(jnp.bfloat16)
    own_start = at_ref[n_slots]

    @pl.when(pl.program_id(0) == own_start // blk)
    def _():
        own_ref[...] = acc_ref[pl.ds(pl.multiple_of(own_start % blk, ROWS), ROWS), :]


def resid_and_hidden(at, x, gain, parts, slots):
    rows = x.shape[0]
    blk = 512
    grid_spec = pltpu.PrefetchScalarGridSpec(
        num_scalar_prefetch=1,
        grid=(rows // blk,),
        in_specs=[pl.BlockSpec((blk, D), lambda i, a: (i, 0)), whole((1, D))]
        + [whole(part.shape) for part in parts]
        + [pl.BlockSpec((blk, slot.shape[1]), lambda i, a: (i, 0)) for slot in slots],
        out_specs=[pl.BlockSpec((blk, D), lambda i, a: (i, 0)), whole((ROWS, D))],
        scratch_shapes=[pltpu.VMEM((blk, D), jnp.float32)],
    )
    return pl.pallas_call(
        functools.partial(resid_kernel, n_parts=len(parts), n_slots=len(slots)),
        grid_spec=grid_spec,
        out_shape=[
            jax.ShapeDtypeStruct((rows, D), jnp.bfloat16),
            jax.ShapeDtypeStruct((ROWS, D), jnp.float32),
        ],
        compiler_params=params(),
        cost_estimate=cost(8.6, 24),
        name="resid_and_hidden",
    )(at, x, gain.reshape(1, D), *parts, *slots)


def strips(width):
    return [slice(at, min(at + 256, width)) for at in range(0, width, 256)]


def forward_kernel(x_ref, gate_w_ref, up_w_ref, act_ref, for_gate_ref, for_up_ref, gate_acc):
    phase = pl.program_id(1)

    @pl.when(phase == 0)
    def _():
        gate_acc[...] = matmul(x_ref[0], gate_w_ref[0])

    @pl.when(phase == 1)
    def _():
        for at in strips(gate_acc.shape[1]):
            up = matmul(x_ref[0], up_w_ref[0, :, at])
            silu, slope = silu_parts(gate_acc[:, at])
            act_ref[0, :, at] = (silu * up).astype(jnp.bfloat16)
            for_gate_ref[0, :, at] = (up * slope).astype(jnp.bfloat16)
            for_up_ref[0, :, at] = silu.astype(jnp.bfloat16)


def per_expert(shape):
    rest = (0,) * (len(shape) - 1)
    return pl.BlockSpec((1,) + shape[1:], lambda e, i: (e,) + rest)


def experts_forward(expert_in, gate, up):
    ff = gate.shape[2]
    hidden = jax.ShapeDtypeStruct((EXP_DEV, CAPB, ff), jnp.bfloat16)
    return pl.pallas_call(
        forward_kernel,
        grid=(EXP_DEV, 2),
        in_specs=[per_expert(expert_in.shape), per_expert(gate.shape), per_expert(up.shape)],
        out_specs=[per_expert(hidden.shape)] * 3,
        out_shape=[hidden] * 3,
        scratch_shapes=[pltpu.VMEM((CAPB, ff), jnp.float32)],
        compiler_params=params(),
        cost_estimate=cost(12, 36),
        name="experts_forward",
    )(expert_in, gate, up)


def backward_kernel(dout_ref, for_gate_ref, for_up_ref, down_ref, gate_ref, up_ref, both_ref, din_ref):
    phase = pl.program_id(1)
    ff = gate_ref.shape[2]

    @pl.when(phase == 0)
    def _():
        for at in strips(ff):
            d_act = times_transposed(dout_ref[0], down_ref[0, at, :])
            for_gate, for_up = for_gate_ref[0, :, at], for_up_ref[0, :, at]
            there = slice(ff + at.start, ff + at.stop)
            both_ref[0, :, at] = (d_act * for_gate.astype(jnp.float32)).astype(jnp.bfloat16)
            both_ref[0, :, there] = (d_act * for_up.astype(jnp.float32)).astype(jnp.bfloat16)

    @pl.when(phase > 0)
    def _():
        for at in strips(gate_ref.shape[1]):
            total = times_transposed(both_ref[0, :, :ff], gate_ref[0, at, :])
            total = total + times_transposed(both_ref[0, :, ff:], up_ref[0, at, :])
            din_ref[0, :, at] = total.astype(jnp.bfloat16)


def experts_backward(d_out, for_gate, for_up, gate, up, down):
    ff = gate.shape[2]
    cols = D // 2
    hidden = (EXP_DEV, CAPB, ff)
    both = (EXP_DEV, CAPB, 2 * ff)
    half_rows = pl.BlockSpec((1, cols, ff), lambda e, i: (e, jnp.maximum(i - 1, 0), 0))
    return pl.pallas_call(
        backward_kernel,
        grid=(EXP_DEV, 3),
        in_specs=[
            per_expert(d_out.shape), per_expert(hidden), per_expert(hidden),
            per_expert(down.shape), half_rows, half_rows,
        ],
        out_specs=[
            per_expert(both),
            pl.BlockSpec((1, CAPB, cols), lambda e, i: (e, 0, jnp.maximum(i - 1, 0))),
        ],
        out_shape=[
            jax.ShapeDtypeStruct(both, jnp.bfloat16),
            jax.ShapeDtypeStruct((EXP_DEV, CAPB, D), jnp.bfloat16),
        ],
        compiler_params=params(),
        cost_estimate=cost(18, 50),
        name="experts_backward",
    )(d_out, for_gate, for_up, down, gate, up)


def out_kernel(act_ref, mass_ref, down_ref, out_ref):
    out_ref[0] = (matmul(act_ref[0], down_ref[0]) * mass_ref[0]).astype(jnp.bfloat16)


def experts_out(act, mass, down):
    ff = act.shape[2]
    cols = D // 2
    return pl.pallas_call(
        out_kernel,
        grid=(EXP_DEV, 2),
        in_specs=[
            per_expert(act.shape), per_expert(mass.shape),
            pl.BlockSpec((1, ff, cols), lambda e, i: (e, 0, i)),
        ],
        out_specs=pl.BlockSpec((1, CAPB, cols), lambda e, i: (e, 0, i)),
        out_shape=jax.ShapeDtypeStruct((EXP_DEV, CAPB, D), jnp.bfloat16),
        compiler_params=params(),
        cost_estimate=cost(1, 4),
        name="experts_out",
    )(act, mass, down)


def products_kernel(*refs):
    out_ref = refs[-1]
    total = None
    for k in range(len(refs) // 2):
        product = matmul(refs[2 * k][...], refs[2 * k + 1][...])
        total = product if total is None else total + product
    out_ref[...] = total.astype(out_ref.dtype)


def sum_of_products(name, terms, gflop, mbytes):
    rows, blk = terms[0][0].shape[0], 512
    specs, flat = [], []
    for left, right in terms:
        specs += [whole(left.shape), pl.BlockSpec((right.shape[0], blk), lambda i: (0, i))]
        flat += [left, right]
    return pl.pallas_call(
        products_kernel,
        grid=(D // blk,),
        in_specs=specs,
        out_specs=pl.BlockSpec((rows, blk), lambda i: (0, i)),
        out_shape=jax.ShapeDtypeStruct((rows, D), jnp.bfloat16),
        compiler_params=params(),
        cost_estimate=cost(gflop / 5, mbytes / 5),
        name=name,
    )(*flat)


def shared_kernel(hidden_ref, dy_ref, gate_ref, up_ref, down_ref, act_ref, d_gate_ref, d_up_ref):
    hidden = hidden_ref[...]
    gate = times_transposed(hidden, gate_ref[...])
    up = times_transposed(hidden, up_ref[...])
    d_act = times_transposed(dy_ref[...], down_ref[...])
    silu, slope = silu_parts(gate)
    act_ref[...] = (silu * up).astype(jnp.bfloat16)
    d_gate_ref[...] = (d_act * up * slope).astype(jnp.bfloat16)
    d_up_ref[...] = (d_act * silu).astype(jnp.bfloat16)


def shared_experts(hidden_in, dy, gate, up, down):
    rows, blk = hidden_in.shape[0], 512
    width = down.shape[0]
    row_spec = lambda size: pl.BlockSpec((blk, size), lambda i: (i, 0))
    return pl.pallas_call(
        shared_kernel,
        grid=(rows // blk,),
        in_specs=[row_spec(D), row_spec(D)] + [whole(down.shape)] * 3,
        out_specs=[row_spec(width)] * 3,
        out_shape=[jax.ShapeDtypeStruct((rows, width), jnp.bfloat16)] * 3,
        compiler_params=params(),
        cost_estimate=cost(4.4, 15),
        name="shared_experts",
    )(hidden_in, dy, gate, up, down)


def parts_kernel(at_ref, *refs, n_terms):
    outs, total_ref = refs[2 * n_terms : -1], refs[-1]
    total = None
    for k in range(n_terms):
        product = matmul(refs[2 * k][...], refs[2 * k + 1][...])
        total = product if total is None else total + product
    total_ref[...] = total.astype(jnp.bfloat16)
    for k, out in enumerate(outs):
        out[...] = total_ref[pl.ds(pl.multiple_of(at_ref[k], ROWS), ROWS), :]


def row_parts(name, at, terms, gflop, mbytes):
    rows, blk = terms[0][0].shape[0], 512
    specs, flat = [], []
    for left, right in terms:
        specs += [
            pl.BlockSpec(left.shape, lambda i, a: (0, 0)),
            pl.BlockSpec((right.shape[0], blk), lambda i, a: (0, i)),
        ]
        flat += [left, right]
    grid_spec = pltpu.PrefetchScalarGridSpec(
        num_scalar_prefetch=1,
        grid=(D // blk,),
        in_specs=specs,
        out_specs=[pl.BlockSpec((ROWS, blk), lambda i, a: (0, i))] * (rows // ROWS),
        scratch_shapes=[pltpu.VMEM((rows, blk), jnp.bfloat16)],
    )
    return pl.pallas_call(
        functools.partial(parts_kernel, n_terms=len(terms)),
        grid_spec=grid_spec,
        out_shape=[jax.ShapeDtypeStruct((ROWS, D), jnp.bfloat16)] * (rows // ROWS),
        compiler_params=params(),
        cost_estimate=cost(gflop / 5, mbytes / 5),
        name=name,
    )(at, *flat)


def latent_kernel(at_ref, dkv_ref, kvw_ref, dkr_ref, *refs):
    outs, tile = refs[:-1], refs[-1]
    tile[:, :RANK] = times_transposed(dkv_ref[...], kvw_ref[...]).astype(jnp.bfloat16)
    tile[:, RANK:] = dkr_ref[...]
    for k, out in enumerate(outs):
        out[0] = tile[pl.ds(pl.multiple_of(at_ref[k], ROWS), ROWS), :]


def latent_parts(at, d_kv, keyval_weight, d_krope, n_ctx):
    blk = d_kv.shape[0] // n_ctx
    row_spec = lambda width: pl.BlockSpec((blk, width), lambda i, a: (i, 0))
    grid_spec = pltpu.PrefetchScalarGridSpec(
        num_scalar_prefetch=1,
        grid=(n_ctx,),
        in_specs=[
            row_spec(d_kv.shape[1]),
            pl.BlockSpec(keyval_weight.shape, lambda i, a: (0, 0)),
            row_spec(128),
        ],
        out_specs=[pl.BlockSpec((1, ROWS, RANK + 128), lambda i, a: (i, 0, 0))] * (blk // ROWS),
        scratch_shapes=[pltpu.VMEM((blk, RANK + 128), jnp.bfloat16)],
    )
    return pl.pallas_call(
        latent_kernel,
        grid_spec=grid_spec,
        out_shape=[jax.ShapeDtypeStruct((n_ctx, ROWS, RANK + 128), jnp.bfloat16)] * (blk // ROWS),
        compiler_params=params(),
        cost_estimate=cost(1, 6),
        name="latent_parts",
    )(at, d_kv, keyval_weight, d_krope)


def turn(values, axis, step):
    size = lax.axis_size(axis)
    return lax.ppermute(values, axis, [(i, (i + step) % size) for i in range(size)])


def move(values, flip):
    pairs = [(i, i ^ flip) for i in range(lax.axis_size("experts"))]
    return lax.ppermute(values, "experts", pairs)


def first_moves(values):
    return move(values, 4), move(values, 2), move(values, 1)


def last_moves(values, first):
    far, near, beside = first
    both = move(far, 2)
    return [values, beside, near, move(near, 1), far, move(far, 1), both, move(both, 1)]


def gather_slots(values):
    return last_moves(values, first_moves(values))


def scatter_sum(parts):
    def pair(k):
        return parts[k].astype(jnp.float32) + move(parts[k + 1], 1).astype(jnp.float32)

    def sent(values, flip):
        return move(values.astype(jnp.bfloat16), flip).astype(jnp.float32)

    both = sent(pair(6), 2)
    far = sent(pair(4) + both, 4)
    near = sent(pair(2), 2)
    return pair(0) + near + far


def butterfly(values, axis):
    size = lax.axis_size(axis)
    span = 1
    while span < size:
        pairs = [(i, i ^ span) for i in range(size)]
        values = values + lax.ppermute(values, axis, pairs)
        span *= 2
    return values


def gather_quarters(shard, dim):
    return lax.all_gather(shard, ("context", "dp"), axis=dim, tiled=True)


def tie(*values):
    return lax.optimization_barrier(values)


def grad_stages(product, split, dim):
    n_ctx, n_dp = lax.axis_size("context"), lax.axis_size("dp")
    my_ctx, my_dp = lax.axis_index("context"), lax.axis_index("dp")
    width = split.shape[2] // (n_ctx * n_dp)
    part = lambda c, d: lax.dynamic_slice_in_dim(split, (c * n_dp + d) * width, width, 2)
    got = []
    for j in range(1, n_dp):
        there = (my_dp + j) % n_dp
        sent = product(jnp.concatenate([part(c, there) for c in range(n_ctx)], 2), slice(None))
        got.append(turn(sent.astype(jnp.bfloat16), "dp", j))

    def near(c, experts):
        total = product(part(c, my_dp)[experts], experts)
        for other in got:
            total = total + lax.dynamic_slice_in_dim(other, c * width, width, dim)[
                experts
            ].astype(jnp.float32)
        return total.astype(jnp.bfloat16)

    sums = [
        [near((my_ctx + k) % n_ctx, slice(e, e + 1)) for k in range(1, n_ctx)]
        for e in range(EXP_DEV)
    ]
    return sums, lambda: near(my_ctx, slice(None))


def send_sums(sums):
    return [[turn(there, "context", k + 1) for k, there in enumerate(some)] for some in sums]


def finish_grad(heard, own):
    own = own.astype(jnp.float32)
    for others in zip(*heard):
        own = own + jnp.concatenate(others, 0).astype(jnp.float32)
    return own


def shared_finish_kernel(first_ref, own_ref, other_ref, gate_ref, up_ref, down_ref):
    width = gate_ref.shape[0]
    swapped = first_ref[0] > 0
    for k, out in enumerate((gate_ref, up_ref, down_ref)):
        own = own_ref[k * width : (k + 1) * width, :].astype(jnp.float32)
        other = other_ref[k * width : (k + 1) * width, :].astype(jnp.float32)
        half = own.shape[1]
        out[:, :half] = jnp.where(swapped, other, own)
        out[:, half:] = jnp.where(swapped, own, other)


def shared_finish(my_dp, own, other):
    rows, half = own.shape
    width = rows // 3
    half_spec = pl.BlockSpec((rows, half), lambda i, a: (0, 0))
    grid_spec = pltpu.PrefetchScalarGridSpec(
        num_scalar_prefetch=1,
        grid=(1,),
        in_specs=[half_spec, half_spec],
        out_specs=[pl.BlockSpec((width, 2 * half), lambda i, a: (0, 0))] * 3,
    )
    return pl.pallas_call(
        shared_finish_kernel,
        grid_spec=grid_spec,
        out_shape=[jax.ShapeDtypeStruct((width, 2 * half), jnp.float32)] * 3,
        compiler_params=params(),
        cost_estimate=cost(0, 13),
        name="shared_finish",
    )(jnp.full((1,), my_dp, jnp.int32), own, other)


def halves_sent(grad, dim):
    n_dp = lax.axis_size("dp")
    my_dp = lax.axis_index("dp")
    width = grad.shape[dim] // n_dp
    part = lambda j: lax.dynamic_slice_in_dim(grad, (my_dp + j) % n_dp * width, width, dim)
    heard = [turn(part(j).astype(jnp.bfloat16), "dp", j) for j in range(1, n_dp)]
    return part(0), heard


def halves_added(own, heard):
    for other in heard:
        own = own + other.astype(jnp.float32)
    return own.astype(jnp.bfloat16)


def context_sent(own):
    return turn(own, "context", 1) if lax.axis_size("context") == 2 else lax.psum(own, "context")


def context_added(own, heard):
    if lax.axis_size("context") != 2:
        return heard
    return (own.astype(jnp.float32) + heard.astype(jnp.float32)).astype(jnp.bfloat16)


def halves_joined(own, dim):
    n_dp = lax.axis_size("dp")
    my_dp = lax.axis_index("dp")
    shape = list(own.shape)
    width = shape[dim]
    shape[dim] = width * n_dp
    total = jnp.zeros(shape, jnp.bfloat16)
    for j in range(n_dp):
        piece = turn(own, "dp", j) if j else own
        at = (my_dp + n_dp - j) % n_dp
        total = lax.dynamic_update_slice_in_dim(total, piece, at * width, dim)
    return total.astype(jnp.float32)


def local(
    layer_input,
    routes,
    route_weights,
    query_weight,
    latent_weight,
    keyval_weight,
    output_weight,
    attn_gain,
    latent_gain,
    ffn_gain,
    shared_gate,
    shared_up,
    shared_down,
    expert_gate,
    expert_up,
    expert_down,
    cotangent,
):
    n_exp = lax.axis_size("experts")
    n_ctx = lax.axis_size("context")
    n_dp = lax.axis_size("dp")
    my_exp = lax.axis_index("experts")
    my_ctx = lax.axis_index("context")
    my_dp = lax.axis_index("dp")
    block_rows = layer_input.shape[2]
    heads_dev = query_weight.shape[1] // (NOPE + ROPE)
    scale = (NOPE + ROPE) ** (-0.5)
    low = jnp.bfloat16
    route_ids = routes.reshape(block_rows, TOPK)
    route_mass = route_weights.reshape(block_rows, TOPK)
    grad_out = cotangent.reshape(block_rows, D)
    own_start = my_exp * ROWS

    def own_rows(values):
        return lax.dynamic_slice_in_dim(values, own_start, ROWS, 0)

    full_gate = gather_quarters(expert_gate, 1)
    full_up = gather_quarters(expert_up, 1)
    full_down = gather_quarters(expert_down, 2)
    lane = jnp.arange(128, dtype=jnp.int32)[None, :]
    freqs = ROPE_BASE ** (-(lane % (ROPE // 2)).astype(jnp.float32) * 2.0 / ROPE)

    def tables(positions):
        turns = positions.astype(jnp.float32)[:, None] * freqs
        sines = jnp.sin(turns)
        sines = jnp.where(lane < ROPE // 2, -sines, sines)
        return (jnp.where(lane < ROPE, jnp.cos(turns), 0.0), jnp.where(lane < ROPE, sines, 0.0))

    query_pos = my_ctx * block_rows + jnp.arange(block_rows, dtype=jnp.int32)
    cos_q, sin_q = tables(query_pos)
    x_block = layer_input.reshape(block_rows, D)
    latent_turned = latent_weight.T
    ow_rows = output_weight.shape[0] // n_dp
    ow_mine = lax.dynamic_slice_in_dim(output_weight, my_dp * ow_rows, ow_rows, 0)
    ow_first = first_moves(ow_mine)
    normed, query, kv_low = front(
        x_block, attn_gain, query_weight, latent_turned, latent_gain, cos_q, sin_q
    )
    kv_low, ow_first = lax.optimization_barrier((kv_low, ow_first))
    ow_slots = last_moves(ow_mine, ow_first)
    kv_all = jnp.zeros((n_ctx * block_rows, RANK + 128), low)
    kv_all = lax.dynamic_update_slice_in_dim(kv_all, kv_low, 0, 0)
    kv_own = own_rows(kv_low)
    kv_heard = []
    for k in range(1, n_ctx):
        pairs = [(i, i + k) for i in range(n_ctx - k)]
        kv_heard.append(lax.ppermute(kv_own, "context", pairs))
    if kv_heard:
        for k, rows in enumerate(gather_slots(jnp.stack(kv_heard))):
            for j in range(n_ctx - 1):
                at = (j + 1) * block_rows + (my_exp ^ k) * ROWS
                kv_all = lax.dynamic_update_slice_in_dim(kv_all, rows[j], at, 0)
    latent_all = kv_all[:, :RANK]
    expanded = matmul(latent_all, keyval_weight).astype(low)
    mixed, logsums = attn_forward(my_ctx, query, expanded, kv_all, scale)

    def head_turn(values, back):
        step = my_dp * VDIM * (heads_dev // n_dp)
        width = values.shape[1]
        twice = jnp.concatenate([values, values], 1)
        start = (width - step) % width if back else step
        return lax.dynamic_slice_in_dim(twice, start, width, 1)

    mixed_turned = head_turn(mixed, False)
    mixed_first = first_moves(mixed_turned)
    mixed_first, ow_slots = lax.optimization_barrier((mixed_first, ow_slots))
    ow_near = jnp.zeros((n_exp, ow_rows, D), low)
    for k, rows in enumerate(ow_slots):
        ow_near = lax.dynamic_update_slice_in_dim(ow_near, rows[None], my_exp ^ k, 0)
    ow_parts = [turn(ow_near, "dp", j) if j else ow_near for j in range(n_dp)]
    mixed_slots = last_moves(mixed_turned, mixed_first)
    slot_at = jnp.stack([my_exp ^ k for k in range(n_exp)] + [own_start]).astype(jnp.int32)
    hidden_in, resid_own = resid_and_hidden(slot_at, x_block, ffn_gain, ow_parts, mixed_slots)
    scale_mid_own = rms_scale(resid_own)

    expert_ids = my_exp * EXP_DEV + jnp.arange(EXP_DEV, dtype=jnp.int32)
    chosen = route_ids[:, :, None] == expert_ids[None, None, :]
    member = jnp.any(chosen, 1)
    mass = jnp.sum(jnp.where(chosen, route_mass[:, :, None], 0.0), 1)
    earlier = (
        jnp.arange(block_rows, dtype=jnp.int32)[:, None]
        > jnp.arange(block_rows, dtype=jnp.int32)[None, :]
    ).astype(low)
    rank = matmul(earlier, member.astype(low)).astype(jnp.int32)
    slot_of = jnp.where(member, rank, -1).T
    taken = slot_of[:, None, :] == jnp.arange(CAPB, dtype=jnp.int32)[None, :, None]
    slot_mass = jnp.sum(jnp.where(taken, mass.T[:, None, :], 0.0), -1)
    pick = taken.astype(low).reshape(EXP_DEV * CAPB, block_rows)
    spread = (
        jnp.where(member, rank, -1)[:, :, None] == jnp.arange(CAPB, dtype=jnp.int32)[None, None, :]
    ).astype(low).reshape(block_rows, EXP_DEV * CAPB)

    d_out = (
        (matmul(pick, grad_out) * slot_mass.reshape(-1, 1)).astype(low).reshape(EXP_DEV, CAPB, D)
    )
    expert_in = matmul(pick, hidden_in).astype(low).reshape(EXP_DEV, CAPB, D)
    act_e, for_gate, for_up = experts_forward(expert_in, full_gate, full_up)
    act_s, d_gate_s, d_up_s = shared_experts(
        hidden_in, grad_out, shared_gate.T, shared_up.T, shared_down
    )
    pool = {}

    def point(name, *carriers):
        extra = {key: value for key, value in pool.items() if PLACES.get(key) == name}
        carriers, extra = lax.optimization_barrier((carriers, extra))
        pool.update(extra)
        return carriers if len(carriers) > 1 else carriers[0]

    slots_all = EXP_DEV * CAPB
    target_rows = jnp.stack([(my_exp ^ k) * ROWS for k in range(n_exp)]).astype(jnp.int32)

    def reduce_rows(name, terms, gflop, mbytes):
        if OFFLOAD[name]:
            return [sum_of_products(name, terms, gflop, mbytes)]
        return list(row_parts(name, target_rows, terms, gflop, mbytes))

    def reduced(parts):
        if len(parts) > 1:
            return scatter_sum(parts)
        return lax.psum_scatter(parts[0], "experts", scatter_dimension=0, tiled=True)

    down_sums, down_rest = grad_stages(
        lambda part, some: jnp.einsum(
            "ecf,ecd->efd", act_e[some], part, preferred_element_type=jnp.float32
        ),
        d_out,
        2,
    )
    d_out, down_sums, act_s = point("back", d_out, down_sums, act_s)
    pool["down0"], pool["down1"] = send_sums(down_sums)
    d_both, d_in_e = experts_backward(d_out, for_gate, for_up, full_gate, full_up, full_down)
    spread = point("spread", spread)
    d_hidden_parts = reduce_rows(
        "d_hidden",
        [
            (d_gate_s, shared_gate.T),
            (d_up_s, shared_up.T),
            (spread, d_in_e.reshape(slots_all, D)),
        ],
        7.3, 16,
    )
    expert_in, d_both, d_hidden_parts = point("both", expert_in, d_both, d_hidden_parts)
    d_hidden_own = reduced(d_hidden_parts)
    both_sums, both_rest = grad_stages(
        lambda part, some: jnp.einsum(
            "ecd,ecf->edf", part, d_both[some], preferred_element_type=jnp.float32
        ),
        expert_in,
        1,
    )
    act_e, both_sums = point("act", act_e, both_sums)
    pool["both0"], pool["both1"] = send_sums(both_sums)
    pool["down_own"], pool["both_own"] = down_rest(), both_rest()
    out_e = experts_out(act_e, slot_mass[:, :, None], full_down)
    d_shared = jnp.concatenate([d_gate_s, d_up_s], 1)
    shared_grads = jnp.concatenate(
        [contract_rows(d_shared, hidden_in), contract_rows(act_s, grad_out)], 0
    )
    pool["shared_own"] = halves_added(*halves_sent(shared_grads, 1))
    out_e = point("ffn", out_e)
    ffn_parts = reduce_rows(
        "ffn_part",
        [(act_s, shared_down), (spread, out_e.reshape(slots_all, D))],
        5.8, 14,
    )
    d_hidden_own, ffn_parts = point("hid", d_hidden_own, ffn_parts)
    pool["ffn_out"] = reduced(ffn_parts)
    d_hidden_own = d_hidden_own.astype(jnp.float32)
    grad_own = own_rows(grad_out).astype(jnp.float32)

    def norm_mid(values_in):
        return values_in * rms_scale(values_in) * ffn_gain

    _, mid_pull = jax.vjp(norm_mid, resid_own)
    d_resid_own = grad_own + mid_pull(d_hidden_own)[0]
    d_ffn_gain = jnp.sum(d_hidden_own * resid_own * scale_mid_own, 0)
    d_resid_low = point("resid", d_resid_own.astype(low))

    d_mixed_parts = [
        times_transposed(d_resid_low, part.reshape(-1, D))
        .astype(low)
        .reshape(ROWS, n_exp, -1)
        .transpose(1, 0, 2)
        for part in ow_parts
    ]
    d_mixed = lax.all_to_all(jnp.concatenate(d_mixed_parts, 2), "experts", 0, 0, tiled=True)
    if OFFLOAD["d_resid"]:
        pool["d_resid"] = lax.all_gather(d_resid_low, "experts", axis=0, tiled=True)
    else:
        pool["d_resid"] = gather_slots(d_resid_low)
    d_mixed = point("mix", d_mixed)
    pool["shared_heard"] = context_sent(pool["shared_own"])
    d_mixed = head_turn(d_mixed.reshape(block_rows, heads_dev * VDIM), True)

    d_query, d_kv, d_krope = attn_backward(
        my_ctx, query, expanded, kv_all, d_mixed, mixed, logsums, cos_q, sin_q, scale
    )
    d_kv = point("kv", d_kv)
    lat_parts = list(latent_parts(target_rows, d_kv, keyval_weight, d_krope, n_ctx))
    head_width = NOPE + ROPE
    d_query_low = jnp.concatenate(
        [d_query[:, 256 * h : 256 * h + head_width] for h in range(heads_dev)], 1
    )
    d_query_low, lat_parts[0] = point("query", d_query_low, lat_parts[0])
    if OFFLOAD["d_norm"]:
        d_norm_part = times_transposed(d_query_low, query_weight).astype(low)
        pool["d_norm"] = lax.psum_scatter(
            d_norm_part, "experts", scatter_dimension=0, tiled=True
        )
    else:
        parts = row_parts("d_norm", target_rows, [(d_query_low, query_weight.T)], 1.6, 8)
        pool["d_norm"] = scatter_sum(parts)
    d_lat_blocks = point("lat", scatter_sum(lat_parts))
    d_comp_own = d_lat_blocks[0]
    for k in range(1, n_ctx):
        pairs = [(i, i - k) for i in range(k, n_ctx)]
        d_comp_own = d_comp_own + lax.ppermute(
            d_lat_blocks[k].astype(low), "context", pairs
        ).astype(jnp.float32)

    own_pos = my_ctx * block_rows + own_start + jnp.arange(ROWS, dtype=jnp.int32)
    cos_k, sin_k = angles(own_pos)
    own_normed = own_rows(normed)

    def latent_fn(comp_rows, lat_gain):
        lat_part = comp_rows[:, :RANK] * rms_scale(comp_rows[:, :RANK]) * lat_gain
        return jnp.concatenate([lat_part, rotate(comp_rows[:, RANK:], cos_k, sin_k)], -1)

    _, kv_pull = jax.vjp(latent_fn, matmul(own_normed, latent_weight), latent_gain)
    d_comp, d_lat_gain = kv_pull(d_comp_own[:, : RANK + ROPE])
    d_comp_low = point("comp", d_comp.astype(low))
    d_norm_own = pool["d_norm"].astype(jnp.float32)
    d_norm_total = d_norm_own + times_transposed(d_comp_low, latent_weight)

    def norm_in(values_in, gain_in):
        return values_in * rms_scale(values_in) * gain_in

    _, in_pull = jax.vjp(norm_in, own_rows(x_block).astype(jnp.float32), attn_gain)
    d_in_rows, d_attn_gain = in_pull(d_norm_total)
    input_grad = (d_resid_own + d_in_rows).reshape(1, 1, ROWS, D)


    ff = expert_gate.shape[2]
    both_own, both_heard = pool["both_own"], [pool["both0"], pool["both1"]]
    gate_heard = [[v[:, :, :ff] for v in some] for some in both_heard]
    up_heard = [[v[:, :, ff:] for v in some] for some in both_heard]
    expert_gate_grad = finish_grad(gate_heard, both_own[:, :, :ff])
    expert_up_grad = finish_grad(up_heard, both_own[:, :, ff:])
    expert_down_grad = finish_grad([pool["down0"], pool["down1"]], pool["down_own"])
    layer_output = (resid_own + pool["ffn_out"].astype(jnp.float32)).astype(low)
    layer_output = layer_output.reshape(1, 1, ROWS, D)

    shared_own = context_added(pool["shared_own"], pool["shared_heard"])
    shared_gate_grad, shared_up_grad, shared_down_grad = shared_finish(
        my_dp, shared_own, turn(shared_own, "dp", 1)
    )
    shared_gate_grad, shared_up_grad = shared_gate_grad.T, shared_up_grad.T

    def weight_grad(product):
        own = halves_added(*halves_sent(product, 0))
        return halves_joined(context_added(own, context_sent(own)), 0)

    query_grad = weight_grad(contract_rows(normed, d_query_low))
    keyval_grad = weight_grad(contract_rows(latent_all, d_kv))
    d_resid_block = pool["d_resid"]
    if not OFFLOAD["d_resid"]:
        slots, d_resid_block = d_resid_block, jnp.zeros((block_rows, D), low)
        for k, rows in enumerate(slots):
            d_resid_block = lax.dynamic_update_slice_in_dim(
                d_resid_block, rows, (my_exp ^ k) * ROWS, 0
            )
    output_grad = weight_grad(contract_rows(mixed, d_resid_block))

    grad_latent = contract_rows(d_comp_low, own_normed)
    lat_half_cols = D // n_dp
    lat_cols = lat_half_cols // n_exp

    def columns(values, at, width):
        return lax.dynamic_slice_in_dim(values, at, width, 1)

    lat_half = columns(grad_latent, my_dp * lat_half_cols, lat_half_cols)
    for j in range(1, n_dp):
        sent = columns(grad_latent, (my_dp + j) % n_dp * lat_half_cols, lat_half_cols)
        lat_half = lat_half + turn(sent.astype(low), "dp", j).astype(jnp.float32)
    lat_half = lat_half.astype(low)
    lat_own = scatter_sum([columns(lat_half, (my_exp ^ k) * lat_cols, lat_cols) for k in range(n_exp)])
    lat_own = point("lat_own", butterfly(lat_own, "context").astype(low))
    lat_half = jnp.zeros((RANK + ROPE, lat_half_cols), low)
    for k, part in enumerate(gather_slots(lat_own)):
        lat_half = lax.dynamic_update_slice_in_dim(lat_half, part, (my_exp ^ k) * lat_cols, 1)
    latent_grad = jnp.zeros((RANK + ROPE, D), low)
    for j in range(n_dp):
        piece = turn(lat_half, "dp", j) if j else lat_half
        at = (my_dp + n_dp - j) % n_dp
        latent_grad = lax.dynamic_update_slice_in_dim(latent_grad, piece, at * lat_half_cols, 1)
    latent_grad = latent_grad.astype(jnp.float32).T

    gains = jnp.concatenate([d_attn_gain, d_lat_gain, d_ffn_gain])
    for axis in ("dp", "context", "experts"):
        gains = butterfly(gains, axis)
    attn_gain_grad = gains[:D]
    latent_gain_grad = gains[D : D + RANK]
    ffn_gain_grad = gains[D + RANK :]
    return (
        layer_output,
        input_grad,
        query_grad,
        latent_grad,
        keyval_grad,
        output_grad,
        attn_gain_grad,
        latent_gain_grad,
        ffn_gain_grad,
        shared_gate_grad,
        shared_up_grad,
        shared_down_grad,
        expert_gate_grad,
        expert_up_grad,
        expert_down_grad,
    )


def solution(mesh):
    in_specs = (
        P("dp", "context", None, None),
        P("dp", "context", None, None),
        P("dp", "context", None, None),
        P(None, "experts"),
        P(),
        P(None, "experts"),
        P("experts", None),
        P(),
        P(),
        P(),
        P(None, "experts"),
        P(None, "experts"),
        P("experts", None),
        P("experts", ("context", "dp"), None),
        P("experts", ("context", "dp"), None),
        P("experts", None, ("context", "dp")),
        P("dp", "context", None, None),
    )
    out_specs = (
        P("dp", "context", "experts", None),
        P("dp", "context", "experts", None),
        P(None, "experts"),
        P(),
        P(None, "experts"),
        P("experts", None),
        P(),
        P(),
        P(),
        P(None, "experts"),
        P(None, "experts"),
        P("experts", None),
        P("experts", ("context", "dp"), None),
        P("experts", ("context", "dp"), None),
        P("experts", None, ("context", "dp")),
    )
    return jax.shard_map(local, mesh=mesh, in_specs=in_specs, out_specs=out_specs, check_vma=False)
```
